512 devices in a mesh: lat: 8 (over z_lo), lon: 64 (over y, x, z_hi, core).
Axes of the slice: x: 4, y: 4, z: 16 (z_hi: 2, z_lo: 8; z = z_hi * 8 + z_lo), core: 2. Of those that a mesh axis runs over, the one named last changes fastest.
Arguments:
- latent: bfloat16 [2, 48, 768, 512], P(None, 'lat', 'lon'), may hold values from -6 to 6
- upstream: bfloat16 [2, 48, 768, 512], P(None, 'lat', 'lon'), may hold values from -6 to 6
- norm_gain: float32 [512], replicated, may hold values from 0.25 to 1.75
- heads_weight: bfloat16 [512, 1536], replicated, may hold values from -0.25 to 0.25
- mixing_weight: bfloat16 [512, 512], replicated, may hold values from -0.25 to 0.25
- bias_table: float32 [3312, 16], replicated, may hold values from -4 to 320
- bias_index: int32 [1, 8, 144, 144], P(None, 'lat'), may hold values from 0 to 3311
- regions: int32 [2, 48, 768], P(None, 'lat', 'lon'), may hold values from 0 to 2
- merge_gain: float32 [2048], replicated, may hold values from 0.25 to 1.75
- merge_weight: bfloat16 [2048, 512], P('lon'), may hold values from -0.125 to 0.125
Outputs:
- merged: bfloat16 [2, 24, 384, 512], P(None, 'lat', 'lon')
- latent_grad: bfloat16 [2, 48, 768, 512], P(None, 'lat', 'lon')
- heads_grad: float32 [512, 1536], P('lon')
- mixing_grad: float32 [512, 512], P('lon')
The draws below stay inside these ranges and needn't reach their ends.
All inputs are finite; a program needn't handle non-finite values.
Results may differ from the reference program's by a relative error of at most 0.015.
Values may be sent and summed in bfloat16 or wider, within the bound.
No kernel may reach another device: no remote copies, remote signals or barrier semaphores. Data moves between devices by JAX's collectives and lax.ppermute only.
A program may use at most 64 MiB of HBM per device.

```python
import jax
import jax.numpy as jnp
from jax import lax

D = 512
HEADS = 16
MERGE_OUT = 512
WIN_LEV = 2
WIN_LAT = 6
WIN_LON = 12
LEVELS = 2
LAT_DEV = 6
LON_DEV = 12
HEAD_DIM = 32
WIN_TOK = 144
BIAS_ROWS = 3312
NLAT = 48
NLON = 768
ALL_TOKENS = 73728
N_LAT = 8
N_LON = 64


def draw_bias_table(key, part):
    key = jax.random.fold_in(key, 7)
    first = jax.random.fold_in(key, 0)
    base_values = jnp.clip(jax.random.normal(first, (BIAS_ROWS, HEADS), jnp.float32), -4.0, 4.0)
    return base_values


def with_ends(drawn, stream_key, smallest, high):
    shape = drawn.shape
    index_at = [jax.random.randint(jax.random.fold_in(stream_key, axis), (), 0, shape[axis]) for axis in range(len(shape))]
    drawn = drawn.at[tuple(index_at)].set(smallest)
    longest = shape.index(max(shape))
    index_at[longest] = (index_at[longest] + 1) % shape[longest]
    return drawn.at[tuple(index_at)].set(high)


def shard_levels(stream_key, shape, cuts, low, high):
    level, own = 1.0, jax.random.fold_in(stream_key, 6)
    for axis_at, blocks in cuts:
        heights = jnp.exp(jax.random.uniform(jax.random.fold_in(own, axis_at), (blocks,), jnp.float32, low / len(cuts), high / len(cuts)))
        level = level * jnp.repeat(heights, shape[axis_at] // blocks).reshape([-1 if axis == axis_at else 1 for axis in range(len(shape))])
    return level


def noise(rng, dims, deviation, limit, cuts=(), dtype=jnp.bfloat16):
    values = deviation * jax.random.normal(rng, dims, jnp.float32)
    if cuts:
        values = values * shard_levels(rng, dims, cuts, -0.22, 0.18)
    return jnp.clip(values, -limit, limit).astype(dtype)


def setup_inputs(seed: int = 0) -> dict:
    key_list = jax.random.split(jax.random.key(seed), 11)
    latent = noise(key_list[0], (LEVELS, NLAT, NLON, D), 1.0, 6.0, ((1, 8), (2, 64)))
    upstream = noise(key_list[1], (LEVELS, NLAT, NLON, D), 1.0, 6.0, ((1, 8), (2, 64)))
    norm_gain = jnp.clip(1.0 + 0.15 * jax.random.normal(key_list[2], (D,), jnp.float32), 0.25, 1.75)
    heads_weight = noise(key_list[3], (D, 3 * D), D ** -0.5, 0.25)
    mixing_weight = noise(key_list[4], (D, D), D ** -0.5, 0.25)
    bias_table = draw_bias_table(jax.random.fold_in(key_list[10], 71), 0)
    bias_index = with_ends(jax.random.randint(key_list[6], (LEVELS // WIN_LEV, NLAT // WIN_LAT, WIN_TOK, WIN_TOK), 0, BIAS_ROWS), jax.random.fold_in(key_list[6], 1), 0, BIAS_ROWS - 1).astype(jnp.int32)
    regions = with_ends(jax.random.randint(key_list[7], (LEVELS, NLAT, NLON), 0, 3), jax.random.fold_in(key_list[7], 1), 0, 2).astype(jnp.int32)
    merge_gain = jnp.clip(1.0 + 0.15 * jax.random.normal(key_list[8], (4 * D,), jnp.float32), 0.25, 1.75)
    merge_weight = noise(key_list[9], (4 * D, MERGE_OUT), (4 * D) ** -0.5, 0.125, ((0, 64),))
    return {"latent": latent, "upstream": upstream, "norm_gain": norm_gain, "heads_weight": heads_weight, "mixing_weight": mixing_weight, "bias_table": bias_table, "bias_index": bias_index, "regions": regions, "merge_gain": merge_gain, "merge_weight": merge_weight}


EPSILON = 1e-05
MASKED = -1e+30

def standardize(values):
    average = lax.optimization_barrier(jnp.mean(values, axis=-1, keepdims=True))
    centred = values - average
    variance = lax.optimization_barrier(jnp.mean(centred * centred, axis=-1, keepdims=True))
    inverse = lax.rsqrt(variance + EPSILON)
    return (centred * inverse, inverse)

def multiply(form, left, right):
    return jnp.einsum(form, left.astype(jnp.float32), right.astype(jnp.float32))

def to_windows(planes):
    level_count, lat_count, lon_count = (planes.shape[0], planes.shape[1], planes.shape[2])
    trailing = planes.shape[3:]
    extra_axes = tuple(range(6, 6 + len(trailing)))
    viewed = planes.reshape((level_count // WIN_LEV, WIN_LEV, lat_count // WIN_LAT, WIN_LAT, lon_count // WIN_LON, WIN_LON) + trailing)
    viewed = viewed.transpose((0, 2, 4, 1, 3, 5) + extra_axes)
    return viewed.reshape((level_count // WIN_LEV, lat_count // WIN_LAT, lon_count // WIN_LON, WIN_TOK) + trailing)

def from_windows(blocks, level_count, lat_count, lon_count):
    trailing = blocks.shape[4:]
    extra_axes = tuple(range(6, 6 + len(trailing)))
    viewed = blocks.reshape((level_count // WIN_LEV, lat_count // WIN_LAT, lon_count // WIN_LON, WIN_LEV, WIN_LAT, WIN_LON) + trailing)
    viewed = viewed.transpose((0, 3, 1, 4, 2, 5) + extra_axes)
    return viewed.reshape((level_count, lat_count, lon_count) + trailing)

def window_pass(normed_band, upstream_band, index_band, group_band, heads_weight, mixing_weight, bias_table):
    level_count, lat_count, lon_count, width = normed_band.shape
    scale = HEAD_DIM ** (-0.5)
    inputs = to_windows(normed_band)
    grads_in = to_windows(upstream_band)
    win_groups = to_windows(group_band[..., None])[..., 0]
    triple = multiply('abcpd,de->abcpe', inputs, heads_weight).astype(jnp.bfloat16)
    head_shape = triple.shape[:4] + (HEADS, HEAD_DIM)
    queries = triple[..., :width].reshape(head_shape)
    keyset = triple[..., width:2 * width].reshape(head_shape)
    valueset = triple[..., 2 * width:].reshape(head_shape)
    raw_scores = multiply('abcqhe,abckhe->abchqk', queries, keyset)
    bias_terms = jnp.take(bias_table, index_band, axis=0)
    bias_terms = jnp.transpose(bias_terms, (0, 1, 4, 2, 3))[:, :, None]
    allowed = (win_groups[..., :, None] == win_groups[..., None, :])[:, :, :, None]
    logits = jnp.where(allowed, raw_scores * scale + bias_terms, MASKED)
    shares = jax.nn.softmax(logits, axis=-1)
    shares_low = shares.astype(jnp.bfloat16)
    context = multiply('abchqk,abckhe->abcqhe', shares_low, valueset).astype(jnp.bfloat16).reshape(inputs.shape)
    attended = multiply('abcpd,de->abcpe', context, mixing_weight).astype(jnp.bfloat16)
    mixing_term = multiply('abcpd,abcpe->de', context, grads_in)
    context_grad = multiply('abcpe,de->abcpd', grads_in, mixing_weight).astype(jnp.bfloat16).reshape(head_shape)
    share_grad = multiply('abcqhe,abckhe->abchqk', context_grad, valueset)
    value_grad = multiply('abchqk,abcqhe->abckhe', shares_low, context_grad)
    logit_grad = (shares * (share_grad - lax.optimization_barrier(jnp.sum(shares * share_grad, axis=-1, keepdims=True)))).astype(jnp.bfloat16)
    query_grad = multiply('abchqk,abckhe->abcqhe', logit_grad, keyset) * scale
    key_grad = multiply('abchqk,abcqhe->abckhe', logit_grad, queries) * scale
    triple_grad = jnp.concatenate([query_grad.reshape(inputs.shape), key_grad.reshape(inputs.shape), value_grad.reshape(inputs.shape)], axis=-1).astype(jnp.bfloat16)
    heads_term = multiply('abcpd,abcpe->de', inputs, triple_grad)
    input_grads = multiply('abcpe,de->abcpd', triple_grad, heads_weight).astype(jnp.bfloat16)
    attended_grid = from_windows(attended, level_count, lat_count, lon_count)
    input_grid = from_windows(input_grads, level_count, lat_count, lon_count)
    return (attended_grid, input_grid, heads_term, mixing_term)

def reference(latent, upstream, norm_gain, heads_weight, mixing_weight, bias_table, bias_index, regions, merge_gain, merge_weight):
    lat_total = LAT_DEV * N_LAT
    lon_total = LON_DEV * N_LON
    band_count = lat_total // WIN_LAT
    latent_f = latent.astype(jnp.float32)
    normalized, inverse = standardize(latent_f)
    normed = (normalized * norm_gain).astype(jnp.bfloat16)
    forward_shift = (-(WIN_LEV // 2), -(WIN_LAT // 2), -(WIN_LON // 2))
    backward_shift = (WIN_LEV // 2, WIN_LAT // 2, WIN_LON // 2)
    normed_shift = jnp.roll(normed, forward_shift, axis=(0, 1, 2))
    upstream_shift = jnp.roll(upstream, forward_shift, axis=(0, 1, 2))
    lat_iota = lax.broadcasted_iota(jnp.int32, regions.shape, 1)
    level_iota = lax.broadcasted_iota(jnp.int32, regions.shape, 0)
    groups = regions + 3 * (lat_iota >= lat_total - WIN_LAT // 2).astype(jnp.int32) + 6 * (level_iota >= LEVELS - WIN_LEV // 2).astype(jnp.int32)

    def banded(planes):
        reshaped = planes.reshape((LEVELS, band_count, WIN_LAT) + planes.shape[2:])
        return jnp.moveaxis(reshaped, 1, 0)

    def unbanded(stacked):
        moved = jnp.moveaxis(stacked, 0, 1)
        return moved.reshape((LEVELS, lat_total) + moved.shape[3:])
    index_bands = jnp.moveaxis(bias_index, 1, 0)[:, :, None]

    def one_band(pieces):
        band_normed, band_upstream, band_index, band_groups = pieces
        return window_pass(band_normed, band_upstream, band_index, band_groups, heads_weight, mixing_weight, bias_table)
    attended_bands, input_bands, heads_terms, mixing_terms = lax.map(one_band, (banded(normed_shift), banded(upstream_shift), index_bands, banded(groups)))
    factor = float(ALL_TOKENS) ** (-0.5)
    heads_grad = lax.optimization_barrier(jnp.sum(heads_terms, axis=0)) * factor
    mixing_grad = lax.optimization_barrier(jnp.sum(mixing_terms, axis=0)) * factor
    attended_back = jnp.roll(unbanded(attended_bands), backward_shift, axis=(0, 1, 2))
    normed_grad = jnp.roll(unbanded(input_bands), backward_shift, axis=(0, 1, 2))
    block_out = (latent_f + attended_back.astype(jnp.float32)).astype(jnp.bfloat16)
    joined = jnp.concatenate([block_out[:, 0::2, 0::2], block_out[:, 1::2, 0::2], block_out[:, 0::2, 1::2], block_out[:, 1::2, 1::2]], axis=-1).astype(jnp.float32)
    merge_norm, unused = standardize(joined)
    features = (merge_norm * merge_gain).astype(jnp.bfloat16)
    flat_features = features.reshape(-1, 4 * D)
    merged = jnp.dot(flat_features, merge_weight, preferred_element_type=jnp.float32).astype(jnp.bfloat16)
    merged = merged.reshape(LEVELS, lat_total // 2, lon_total // 2, MERGE_OUT)
    scaled_grad = normed_grad.astype(jnp.float32) * norm_gain
    first_mean = lax.optimization_barrier(jnp.mean(scaled_grad, axis=-1, keepdims=True))
    second_mean = lax.optimization_barrier(jnp.mean(scaled_grad * normalized, axis=-1, keepdims=True))
    norm_back = inverse * (scaled_grad - first_mean - normalized * second_mean)
    latent_grad = (upstream.astype(jnp.float32) + norm_back).astype(jnp.bfloat16)
    return (merged, latent_grad, heads_grad, mixing_grad)
```

```python
import functools

import jax
import jax.numpy as jnp
from jax import lax
from jax.experimental import pallas as pl
from jax.experimental.pallas import tpu as pltpu
from jax.sharding import PartitionSpec as P

HEADS = 16
HEAD_DIM = 32
LEVELS = 2
WIN_LAT = 6
WIN_LON = 12
TOK = 144
PART = 36
SLOT = 40
EPSILON = 1e-05
MASKED = -1e30
F32, BF16 = jnp.float32, jnp.bfloat16
VMEM = pl.BlockSpec(memory_space=pltpu.VMEM)
SMEM = pl.BlockSpec(memory_space=pltpu.SMEM)


def nn(a, b):
    return lax.dot_general(a, b, (((1,), (0,)), ((), ())), preferred_element_type=F32)


def nt(a, b):
    return lax.dot_general(a, b, (((1,), (1,)), ((), ())), preferred_element_type=F32)


def layer_norm(values):
    average = jnp.mean(values, axis=-1, keepdims=True)
    centred = values - average
    variance = jnp.mean(centred * centred, axis=-1, keepdims=True)
    inverse = lax.rsqrt(variance + EPSILON)
    return centred * inverse, inverse


def one_hot(source, old):
    return jnp.where(source == old, 1.0, 0.0).astype(BF16)


def cell_of_slot(row, level_swap):
    quarter, cell = row // SLOT, row % SLOT
    level, rest = cell // 18, cell % 18
    lat = 3 * (quarter // 2) + rest // 6
    lon = 6 * (quarter % 2) + rest % 6
    if level_swap:
        level = 1 - level
    return jnp.where(cell < PART, level * 72 + lat * 12 + lon, -1)


def slots_from_cells(level_swap=False):
    row = lax.broadcasted_iota(jnp.int32, (4 * SLOT, TOK), 0)
    column = lax.broadcasted_iota(jnp.int32, (4 * SLOT, TOK), 1)
    return one_hot(cell_of_slot(row, level_swap), column)


def cells_from_slots(level_swap=False):
    row = lax.broadcasted_iota(jnp.int32, (TOK, 4 * SLOT), 0)
    column = lax.broadcasted_iota(jnp.int32, (TOK, 4 * SLOT), 1)
    return one_hot(cell_of_slot(column, level_swap), row)


def quarter_of(values, quarter):
    return values[SLOT * quarter : SLOT * quarter + PART].astype(BF16)


def fill_slots(slots_ref, pieces):
    slots_ref[...] = jnp.zeros(slots_ref.shape, F32)
    for quarter, piece in enumerate(pieces):
        slots_ref[SLOT * quarter : SLOT * quarter + PART, :] = piece.astype(F32)
    return slots_ref[...].astype(BF16)


def prepare_kernel(x_ref, u_ref, lon_ref, lat_ref, stay_ref):
    order = slots_from_cells(True)
    for array, ref in enumerate((x_ref, u_ref)):
        values = nn(order, ref[...])
        lon_ref[0, array] = quarter_of(values, 0)
        lon_ref[1, array] = quarter_of(values, 2)
        lat_ref[array] = quarter_of(values, 1)
        stay_ref[array] = quarter_of(values, 3)


def prepare(x, u):
    width = x.shape[1]
    return pl.pallas_call(
        prepare_kernel,
        out_shape=(
            jax.ShapeDtypeStruct((2, 2, PART, width), BF16),
            jax.ShapeDtypeStruct((2, PART, width), BF16),
            jax.ShapeDtypeStruct((2, PART, width), BF16),
        ),
        in_specs=[VMEM] * 2,
        out_specs=(VMEM,) * 3,
        name="prepare",
    )(x, u)


def bias_kernel(index_ref, table_ref, key_group_ref, query_group_ref, bias_ref):
    chunks = table_ref.shape[1] // 128

    def rows(step, carry):
        base = pl.multiple_of(step * 8, 8)
        key_group = key_group_ref[pl.ds(base, 8), :]
        for start, width in ((0, 128), (128, TOK - 128)):
            index = index_ref[pl.ds(base, 8), start : start + 128]
            high = index >> 7
            low = index & 127
            allowed = key_group == query_group_ref[:, start : start + 128]
            found = [jnp.zeros((8, 128), F32) for _ in range(HEADS)]
            for chunk in range(chunks):
                here = high == chunk
                for head in range(HEADS):
                    row = table_ref[head : head + 1, chunk * 128 : chunk * 128 + 128]
                    row = jnp.broadcast_to(row, (8, 128))
                    value = jnp.take_along_axis(row, low, axis=1, mode="promise_in_bounds")
                    found[head] = jnp.where(here, value, found[head])
            for head in range(HEADS):
                masked = jnp.where(allowed, found[head], MASKED)
                bias_ref[head, pl.ds(base, 8), start : start + width] = masked[:, :width]
        return carry

    lax.fori_loop(0, TOK // 8, rows, 0)


def gather_bias(bias_table, bias_index, groups):
    rows = bias_table.shape[0]
    padded = -(-rows // 128) * 128
    table = jnp.pad(bias_table.T, ((0, 0), (0, padded - rows)))
    index = jnp.pad(bias_index.reshape(TOK, TOK).T, ((0, 0), (0, 256 - TOK)))
    flat = groups.reshape(TOK)
    key_group = jnp.broadcast_to(flat[:, None], (TOK, 128))
    query_group = jnp.pad(flat, (0, 256 - TOK))[None]
    return pl.pallas_call(
        bias_kernel,
        out_shape=jax.ShapeDtypeStruct((HEADS, TOK, TOK), F32),
        in_specs=[VMEM] * 4,
        out_specs=VMEM,
        compiler_params=pltpu.CompilerParams(vmem_limit_bytes=32 * 1024 * 1024),
        name="bias_gather",
    )(index, table, key_group, query_group)


def attention_kernel(
    core_ref,
    stay_ref,
    lon_ref,
    lat_ref,
    gain_ref,
    w_ref,
    wt_ref,
    m_ref,
    bias_ref,
    lat_out_ref,
    lon_out_ref,
    stay_out_ref,
    keep_ref,
    send_ref,
    ct_ref,
    dqt_ref,
    tg_ref,
    slots_ref,
):
    width = gain_ref.shape[1]
    scale = HEAD_DIM ** (-0.5)
    core = core_ref[0]
    gather = cells_from_slots()
    arrays = []
    for array in range(2):
        pieces = (stay_ref[array], lon_ref[1, array], lat_ref[0, array], lat_ref[1, array])
        arrays.append(nn(gather, fill_slots(slots_ref, pieces)).astype(BF16))
    x, u = arrays
    standard, _ = layer_norm(x.astype(F32))
    xn = (standard * gain_ref[...]).astype(BF16)
    w = w_ref[...]
    wt = wt_ref[...]
    m = m_ref[...]
    q_nat = nn(xn, w[:, :width]).astype(BF16)
    k_nat = nn(xn, w[:, width : 2 * width]).astype(BF16)
    v_nat = nn(xn, w[:, 2 * width :]).astype(BF16)
    qt = nt(wt[:width], xn).astype(BF16)
    kt = nt(wt[width : 2 * width], xn).astype(BF16)
    vt = nt(wt[2 * width :], xn).astype(BF16)
    cg_nat = nt(u, m).astype(BF16)
    cgt = nt(m, u).astype(BF16)
    lane = lax.broadcasted_iota(jnp.int32, (TOK, 128), 1)
    for group in range(HEADS // 4):
        cut = slice(128 * group, 128 * group + 128)
        kg, vg, qg, cgg = k_nat[:, cut], v_nat[:, cut], q_nat[:, cut], cg_nat[:, cut]
        qtg, cgtg = qt[cut], cgt[cut]
        dk = jnp.zeros((TOK, 128), F32)
        dv = jnp.zeros((TOK, 128), F32)
        for part in range(4):
            head = 4 * group + part
            own = (lane >= HEAD_DIM * part) & (lane < HEAD_DIM * (part + 1))

            def only(block):
                return jnp.where(own, block.astype(F32), 0.0).astype(BF16)

            at = slice(HEAD_DIM * head, HEAD_DIM * head + HEAD_DIM)
            logits = nn(only(kg), qtg) * scale + bias_ref[head]
            top = jnp.max(logits, axis=0, keepdims=True)
            raised = jnp.exp(logits - top)
            shares = raised * (1.0 / jnp.sum(raised, axis=0, keepdims=True))
            shares_low = shares.astype(BF16)
            ct_ref[at, :] = nn(vt[at], shares_low).astype(BF16)
            share_grad = nn(only(vg), cgtg)
            product = shares * share_grad
            total = jnp.sum(product, axis=0, keepdims=True)
            logit_grad = (shares * (share_grad - total)).astype(BF16)
            dqt_ref[at, :] = (nn(kt[at], logit_grad) * scale).astype(BF16)
            dv = dv + nn(shares_low, only(cgg))
            dk = dk + nn(logit_grad, only(qg))
        tg_ref[:, width + 128 * group : width + 128 * group + 128] = (dk * scale).astype(BF16)
        tg_ref[:, 2 * width + 128 * group : 2 * width + 128 * group + 128] = dv.astype(BF16)
    row = lax.broadcasted_iota(jnp.int32, (TOK, TOK), 0)
    column = lax.broadcasted_iota(jnp.int32, (TOK, TOK), 1)
    eye = one_hot(row, column)
    tg_ref[:, :width] = nt(eye, dqt_ref[...]).astype(BF16)
    ct = ct_ref[...]
    context = nt(eye, ct).astype(BF16)
    tg = tg_ref[...]
    spread = slots_from_cells()
    for array, values in enumerate((nn(context, m), nn(tg, wt))):
        values = nn(spread, values.astype(BF16))
        stay_out_ref[array] = quarter_of(values, 0)
        lon_out_ref[array] = quarter_of(values, 1)
        lat_out_ref[0, array] = quarter_of(values, 2)
        lat_out_ref[1, array] = quarter_of(values, 3)
    half = width // 2
    new = lax.broadcasted_iota(jnp.int32, (width, width), 0)
    old = lax.broadcasted_iota(jnp.int32, (width, width), 1)
    local = new & (half - 1)
    parity = jnp.where(new >= half, 1 - core, core)
    order = one_hot(((local >> 3) << 4) + (parity << 3) + (local & 7), old)
    xnt = nt(order, xn).astype(BF16)
    cto = nn(order, ct).astype(BF16)
    for rows, target in ((slice(0, half), keep_ref), (slice(half, width), send_ref)):
        target[:, : 3 * width] = nn(xnt[rows], tg).astype(BF16)
        target[:, 3 * width :] = nn(cto[rows], u).astype(BF16)


def attention(core, stay, lon, lat, gain, w, m, bias):
    width = gain.shape[1]
    return pl.pallas_call(
        attention_kernel,
        out_shape=(
            jax.ShapeDtypeStruct((2, 2, PART, width), BF16),
            jax.ShapeDtypeStruct((2, PART, width), BF16),
            jax.ShapeDtypeStruct((2, PART, width), BF16),
            jax.ShapeDtypeStruct((width // 2, 4 * width), BF16),
            jax.ShapeDtypeStruct((width // 2, 4 * width), BF16),
        ),
        in_specs=[SMEM] + [VMEM] * 8,
        out_specs=(VMEM,) * 5,
        scratch_shapes=[
            pltpu.VMEM((width, TOK), BF16),
            pltpu.VMEM((width, TOK), BF16),
            pltpu.VMEM((TOK, 3 * width), BF16),
            pltpu.VMEM((4 * SLOT, width), F32),
        ],
        compiler_params=pltpu.CompilerParams(vmem_limit_bytes=40 * 1024 * 1024),
        name="window_attention",
    )(core, stay, lon, lat, gain, w, w.T, m, bias)


def finish_kernel(
    x_ref,
    u_ref,
    stay_ref,
    lat_ref,
    lon_ref,
    gain_ref,
    merge_gain_ref,
    merge_weight_ref,
    grad_ref,
    merged_ref,
    slots_ref,
):
    width = x_ref.shape[1]
    x = x_ref[...]
    gather = cells_from_slots(True)
    arrays = []
    for array in range(2):
        pieces = (lon_ref[1, array], lat_ref[array], lon_ref[0, array], stay_ref[array])
        arrays.append(fill_slots(slots_ref, pieces))
    gain = gain_ref[...]
    normalized, inverse = layer_norm(x.astype(F32))
    scaled = nn(gather, arrays[1]) * gain
    first = jnp.mean(scaled, axis=-1, keepdims=True)
    second = jnp.mean(scaled * normalized, axis=-1, keepdims=True)
    back = inverse * (scaled - first - normalized * second)
    grad_ref[...] = (u_ref[...].astype(F32) + back).astype(BF16)
    block = (x.astype(F32) + nn(gather, arrays[0])).astype(BF16)
    row = lax.broadcasted_iota(jnp.int32, (4 * SLOT, TOK), 0)
    column = lax.broadcasted_iota(jnp.int32, (4 * SLOT, TOK), 1)
    corner, cell = row // SLOT, row % SLOT
    level, rest = cell // 18, cell % 18
    place = level * 72 + (2 * (rest // 6) + corner % 2) * 12 + 2 * (rest % 6) + corner // 2
    corners = nn(one_hot(jnp.where(cell < PART, place, -1), column), block)
    joined = jnp.concatenate([corners[SLOT * c : SLOT * c + SLOT] for c in range(4)], axis=-1)
    features, _ = layer_norm(joined)
    features = (features * merge_gain_ref[...]).astype(BF16)
    merged_ref[...] = nn(features, merge_weight_ref[...])[:PART].astype(BF16)


def finish(x, u, stay, lat, lon, gain, merge_gain, merge_weight):
    width = x.shape[1]
    return pl.pallas_call(
        finish_kernel,
        out_shape=(
            jax.ShapeDtypeStruct((TOK, width), BF16),
            jax.ShapeDtypeStruct((PART, merge_weight.shape[1]), BF16),
        ),
        in_specs=[VMEM] * 8,
        out_specs=(VMEM,) * 2,
        scratch_shapes=[pltpu.VMEM((4 * SLOT, width), F32)],
        compiler_params=pltpu.CompilerParams(vmem_limit_bytes=32 * 1024 * 1024),
        name="finish",
    )(x, u, stay, lat, lon, gain, merge_gain, merge_weight)


def shifted(array, axis, by):
    size = lax.axis_size(axis)
    return lax.ppermute(array, axis, [(i, (i + by) % size) for i in range(size)])


def exchanged(array, axes, groups):
    return lax.all_to_all(array, axes, 0, 0, axis_index_groups=groups, tiled=True)


def reduce_rows(keep, send):
    lon_size, lat_size = lax.axis_size("lon"), lax.axis_size("lat")
    columns = keep.shape[1]
    arrived = lax.ppermute(send, "lon", [(i, i ^ 1) for i in range(lon_size)])
    paired = (keep.astype(F32) + arrived.astype(F32)).astype(BF16)
    plane = lon_size // 4
    groups = [[4 * j + r for j in range(plane)] for r in range(4)]
    terms = exchanged(paired, "lon", groups).reshape(plane, -1, columns)
    planes = jnp.sum(terms.astype(F32), axis=0).astype(BF16)
    groups = [
        [level * lon_size + o + 2 * high for high in range(2) for level in range(lat_size)]
        for o in range(lon_size)
        if not o & 2
    ]
    rows = planes.shape[0] // (2 * lat_size)
    terms = exchanged(planes, ("lat", "lon"), groups).reshape(2 * lat_size, rows, columns)
    row = jnp.sum(terms.astype(F32), axis=0).astype(BF16)
    copies = jnp.broadcast_to(row[None], (lat_size,) + row.shape).reshape(-1, columns)
    return exchanged(copies, "lat", None)


def on_device(
    latent,
    upstream,
    norm_gain,
    heads_weight,
    mixing_weight,
    bias_table,
    bias_index,
    regions,
    merge_gain,
    merge_weight,
):
    level_count, lat_count, lon_count, width = latent.shape
    lat_total = lat_count * lax.axis_size("lat")
    token_total = level_count * lat_total * lon_count * lax.axis_size("lon")
    factor = float(token_total) ** (-0.5)
    whole_merge = lax.all_gather(merge_weight, "lon", axis=0, tiled=True)
    x = latent.reshape(TOK, width)
    u = upstream.reshape(TOK, width)
    lon_half, lat_half, stay = prepare(x, u)
    lon_half = shifted(lon_half, "lon", -1)
    lat_half = shifted(jnp.stack([lat_half, lon_half[0]]), "lat", -1)
    lat_global = lax.axis_index("lat") * lat_count + lax.broadcasted_iota(
        jnp.int32, regions.shape, 1
    )
    level_local = lax.broadcasted_iota(jnp.int32, regions.shape, 0)
    groups = (
        regions
        + 3 * (lat_global >= lat_total - WIN_LAT // 2).astype(jnp.int32)
        + 6 * (level_local >= LEVELS - 1).astype(jnp.int32)
    )
    bias = gather_bias(bias_table, bias_index, groups)
    core = (lax.axis_index("lon") % 2).astype(jnp.int32).reshape(1)
    gain = norm_gain[None]
    lat_back, lon_back, stay_back, keep, send = attention(
        core, stay, lon_half, lat_half, gain, heads_weight, mixing_weight, bias
    )
    lat_back = shifted(lat_back, "lat", 1)
    lon_back = shifted(jnp.stack([lon_back, lat_back[1]]), "lon", 1)
    rows = reduce_rows(keep, send).astype(F32) * factor
    latent_grad, merged = finish(
        x, u, stay_back, lat_back[0], lon_back, gain, merge_gain[None], whole_merge
    )
    merged = merged.reshape(level_count, lat_count // 2, lon_count // 2, -1)
    return merged, latent_grad.reshape(latent.shape), rows[:, : 3 * width], rows[:, 3 * width :]


def solution(mesh):
    placed = (
        P(None, "lat", "lon", None),
        P(None, "lat", "lon", None),
        P(),
        P(),
        P(),
        P(),
        P(None, "lat", None, None),
        P(None, "lat", "lon"),
        P(),
        P("lon", None),
    )
    return jax.shard_map(
        on_device,
        mesh=mesh,
        in_specs=placed,
        out_specs=(
            P(None, "lat", "lon", None),
            P(None, "lat", "lon", None),
            P("lon", None),
            P("lon", None),
        ),
        check_vma=False,
    )
```

```python
import functools

import jax
import jax.numpy as jnp
from jax import lax
from jax.experimental import pallas as pl
from jax.experimental.pallas import tpu as pltpu
from jax.sharding import PartitionSpec as P

HEADS = 16
HEAD_DIM = 32
LEVELS = 2
WIN_LAT = 6
WIN_LON = 12
TOK = 144
PART = 36
SLOT = 40
EPSILON = 1e-05
MASKED = -1e30
F32, BF16 = jnp.float32, jnp.bfloat16
VMEM = pl.BlockSpec(memory_space=pltpu.VMEM)
SMEM = pl.BlockSpec(memory_space=pltpu.SMEM)


def nn(a, b):
    return lax.dot_general(a, b, (((1,), (0,)), ((), ())), preferred_element_type=F32)


def nt(a, b):
    return lax.dot_general(a, b, (((1,), (1,)), ((), ())), preferred_element_type=F32)


def layer_norm(values):
    average = jnp.mean(values, axis=-1, keepdims=True)
    centred = values - average
    variance = jnp.mean(centred * centred, axis=-1, keepdims=True)
    inverse = lax.rsqrt(variance + EPSILON)
    return centred * inverse, inverse


def one_hot(source, old):
    return jnp.where(source == old, 1.0, 0.0).astype(BF16)


def cell_of_slot(row, level_swap):
    quarter, cell = row // SLOT, row % SLOT
    level, rest = cell // 18, cell % 18
    lat = 3 * (quarter // 2) + rest // 6
    lon = 6 * (quarter % 2) + rest % 6
    if level_swap:
        level = 1 - level
    return jnp.where(cell < PART, level * 72 + lat * 12 + lon, -1)


def slots_from_cells(level_swap=False):
    row = lax.broadcasted_iota(jnp.int32, (4 * SLOT, TOK), 0)
    column = lax.broadcasted_iota(jnp.int32, (4 * SLOT, TOK), 1)
    return one_hot(cell_of_slot(row, level_swap), column)


def cells_from_slots(level_swap=False):
    row = lax.broadcasted_iota(jnp.int32, (TOK, 4 * SLOT), 0)
    column = lax.broadcasted_iota(jnp.int32, (TOK, 4 * SLOT), 1)
    return one_hot(cell_of_slot(column, level_swap), row)


def quarters_of(values):
    return [values[SLOT * q : SLOT * q + SLOT] for q in range(4)]


def stacked(pieces):
    return jnp.concatenate(pieces, axis=0).astype(BF16)


def row_of_place(place):
    level, rest = place // (TOK // 2), place % (TOK // 2)
    return jnp.where(place < 0, -1, 2 * rest + level)


def prepare_kernel(x_ref, u_ref, lon_ref, lat_ref, stay_ref):
    row = lax.broadcasted_iota(jnp.int32, (4 * SLOT, TOK), 0)
    column = lax.broadcasted_iota(jnp.int32, (4 * SLOT, TOK), 1)
    order = one_hot(row_of_place(cell_of_slot(row, True)), column)
    x = quarters_of(nn(order, x_ref[...]))
    u = quarters_of(nn(order, u_ref[...]))
    lon_ref[...] = stacked([x[0], u[0], x[2], u[2]])
    lat_ref[...] = stacked([x[1], u[1]])
    stay_ref[...] = stacked([x[3], u[3]])


def prepare(x, u):
    width = x.shape[-1]
    return pl.pallas_call(
        prepare_kernel,
        out_shape=(
            jax.ShapeDtypeStruct((4 * SLOT, width), BF16),
            jax.ShapeDtypeStruct((2 * SLOT, width), BF16),
            jax.ShapeDtypeStruct((2 * SLOT, width), BF16),
        ),
        in_specs=[VMEM] * 2,
        out_specs=(VMEM,) * 3,
        name="prepare",
    )(x, u)


def lookup(index, table_ref):
    high, low = index >> 7, index & 127
    found = [jnp.zeros(index.shape, F32) for _ in range(HEADS)]
    for chunk in range(table_ref.shape[1] // 128):
        here = high == chunk
        for head in range(HEADS):
            row = table_ref[head : head + 1, chunk * 128 : chunk * 128 + 128]
            row = jnp.broadcast_to(row, index.shape)
            value = jnp.take_along_axis(row, low, axis=1, mode="promise_in_bounds")
            found[head] = jnp.where(here, value, found[head])
    return found


def bias_kernel(index_ref, table_ref, key_group_ref, query_group_ref, bias_ref, tail_ref):
    rest = TOK - 128
    per_row = 128 // rest

    def allowed(base, start):
        return key_group_ref[pl.ds(base, 8), :] == query_group_ref[:, start : start + 128]

    def main_rows(step, carry):
        base = pl.multiple_of(step * 8, 8)
        open_pairs = allowed(base, 0)
        for head, value in enumerate(lookup(index_ref[pl.ds(base, 8), :], table_ref)):
            bias_ref[head, pl.ds(base, 8), :128] = jnp.where(open_pairs, value, MASKED)
        return carry

    def tail_rows(step, carry):
        base = pl.multiple_of(step * 8, 8)
        for head, value in enumerate(lookup(index_ref[pl.ds(TOK + base, 8), :], table_ref)):
            tail_ref[head, pl.ds(base, 8), :] = value
        return carry

    def spread_rows(step, carry):
        base = pl.multiple_of(step * 8, 8)
        open_pairs = allowed(base, 128)
        sublane = lax.broadcasted_iota(jnp.int32, (8, 128), 0)
        lane = lax.broadcasted_iota(jnp.int32, (8, 128), 1)
        place = sublane * rest + (lane & (rest - 1))
        for head in range(HEADS):
            row = jnp.broadcast_to(tail_ref[head, pl.ds(step, 1), :], (8, 128))
            value = jnp.take_along_axis(row, place, axis=1, mode="promise_in_bounds")
            value = jnp.where(open_pairs, value, MASKED)
            bias_ref[head, pl.ds(base, 8), 128:] = value[:, :rest]
        return carry

    lax.fori_loop(0, TOK // 8, main_rows, 0)
    lax.fori_loop(0, tail_ref.shape[1] // 8, tail_rows, 0)
    lax.fori_loop(0, TOK // per_row, spread_rows, 0)


def bias_operands(bias_table, bias_index, groups):
    rows = bias_table.shape[0]
    padded = -(-rows // 128) * 128
    table = jnp.pad(bias_table.T, ((0, 0), (0, padded - rows)))
    index = bias_index.reshape(TOK, TOK).T
    tail = index[:, 128:].reshape(-1, 128)
    tail = jnp.pad(tail, ((0, -tail.shape[0] % 8), (0, 0)))
    index = jnp.concatenate([index[:, :128], tail])
    flat = groups.reshape(TOK)
    key_group = jnp.broadcast_to(flat[:, None], (TOK, 128))
    query_group = jnp.pad(flat, (0, 256 - TOK))[None]
    return index, table, key_group, query_group


def gather_bias(operands):
    tail = operands[0].shape[0] - TOK
    return pl.pallas_call(
        bias_kernel,
        out_shape=jax.ShapeDtypeStruct((HEADS, TOK, TOK), F32),
        in_specs=[VMEM] * 4,
        out_specs=VMEM,
        scratch_shapes=[pltpu.VMEM((HEADS, tail, 128), F32)],
        compiler_params=pltpu.CompilerParams(vmem_limit_bytes=12 * 1024 * 1024),
        name="bias_gather",
    )(*operands)


def attention_kernel(
    core_ref,
    stay_ref,
    lon_ref,
    lat_ref,
    gain_ref,
    w_ref,
    m_ref,
    bias_ref,
    lat_out_ref,
    lon_out_ref,
    stay_out_ref,
    keep_ref,
    send_ref,
    ct_ref,
    dqt_ref,
    tg_ref,
):
    width = gain_ref.shape[1]
    scale = HEAD_DIM ** (-0.5)
    core = core_ref[0]
    gather = cells_from_slots()
    stay, lon, lat = (r[...].astype(F32) for r in (stay_ref, lon_ref, lat_ref))
    arrays = []
    for array in range(2):
        at = slice(SLOT * array, SLOT * array + SLOT)
        later = slice(SLOT * array + 2 * SLOT, SLOT * array + 3 * SLOT)
        slots = stacked([stay[at], lon[later], lat[at], lat[later]])
        arrays.append(nn(gather, slots).astype(BF16))
    x, u = arrays
    standard, _ = layer_norm(x.astype(F32))
    xn = (standard * gain_ref[...]).astype(BF16)
    w = w_ref[...]
    m = m_ref[...]
    q_nat = nn(xn, w[:, :width]).astype(BF16)
    k_nat = nn(xn, w[:, width : 2 * width]).astype(BF16)
    v_nat = nn(xn, w[:, 2 * width :]).astype(BF16)
    row = lax.broadcasted_iota(jnp.int32, (width, width), 0)
    column = lax.broadcasted_iota(jnp.int32, (width, width), 1)
    wide_eye = one_hot(row, column)
    qt, kt, vt = (nt(wide_eye, block).astype(BF16) for block in (q_nat, k_nat, v_nat))
    cg_nat = nt(u, m).astype(BF16)
    cgt = nt(m, u).astype(BF16)
    lane = lax.broadcasted_iota(jnp.int32, (TOK, 128), 1)
    for group in range(HEADS // 4):
        cut = slice(128 * group, 128 * group + 128)
        kg, vg, qg, cgg = k_nat[:, cut], v_nat[:, cut], q_nat[:, cut], cg_nat[:, cut]
        qtg, cgtg = qt[cut], cgt[cut]
        dk = jnp.zeros((TOK, 128), F32)
        dv = jnp.zeros((TOK, 128), F32)
        for part in range(4):
            head = 4 * group + part
            own = (lane >= HEAD_DIM * part) & (lane < HEAD_DIM * (part + 1))

            def only(block):
                return jnp.where(own, block.astype(F32), 0.0).astype(BF16)

            at = slice(HEAD_DIM * head, HEAD_DIM * head + HEAD_DIM)
            logits = nn(only(kg), qtg) * scale + bias_ref[head]
            top = jnp.max(logits, axis=0, keepdims=True)
            raised = jnp.exp(logits - top)
            shares = raised * (1.0 / jnp.sum(raised, axis=0, keepdims=True))
            shares_low = shares.astype(BF16)
            ct_ref[at, :] = nn(vt[at], shares_low).astype(BF16)
            share_grad = nn(only(vg), cgtg)
            product = shares * share_grad
            total = jnp.sum(product, axis=0, keepdims=True)
            logit_grad = (shares * (share_grad - total)).astype(BF16)
            dqt_ref[at, :] = (nn(kt[at], logit_grad) * scale).astype(BF16)
            dv = dv + nn(shares_low, only(cgg))
            dk = dk + nn(logit_grad, only(qg))
        tg_ref[:, width + 128 * group : width + 128 * group + 128] = (dk * scale).astype(BF16)
        tg_ref[:, 2 * width + 128 * group : 2 * width + 128 * group + 128] = dv.astype(BF16)
    row = lax.broadcasted_iota(jnp.int32, (TOK, TOK), 0)
    column = lax.broadcasted_iota(jnp.int32, (TOK, TOK), 1)
    eye = one_hot(row, column)
    tg_ref[:, :width] = nt(eye, dqt_ref[...]).astype(BF16)
    ct = ct_ref[...]
    context = nt(eye, ct).astype(BF16)
    tg = tg_ref[...]
    spread = slots_from_cells()
    back = [quarters_of(nn(spread, v.astype(BF16))) for v in (nn(context, m), nt(tg, w))]
    stay_out_ref[...] = stacked([back[0][0], back[1][0]])
    lon_out_ref[...] = stacked([back[0][1], back[1][1], back[0][3], back[1][3]])
    lat_out_ref[...] = stacked([back[0][2], back[1][2]])
    half = width // 2
    new = lax.broadcasted_iota(jnp.int32, (width, width), 0)
    old = lax.broadcasted_iota(jnp.int32, (width, width), 1)
    local = new & (half - 1)
    parity = jnp.where(new >= half, 1 - core, core)
    order = one_hot(((local >> 3) << 4) + (parity << 3) + (local & 7), old)
    xnt = nt(order, xn).astype(BF16)
    cto = nn(order, ct).astype(BF16)
    for rows, target in ((slice(0, half), keep_ref), (slice(half, width), send_ref)):
        target[:, : 3 * width] = nn(xnt[rows], tg).astype(BF16)
        target[:, 3 * width :] = nn(cto[rows], u).astype(BF16)


def attention(core, stay, lon, lat, gain, w, m, bias):
    width = gain.shape[1]
    return pl.pallas_call(
        attention_kernel,
        out_shape=(
            jax.ShapeDtypeStruct((2 * SLOT, width), BF16),
            jax.ShapeDtypeStruct((4 * SLOT, width), BF16),
            jax.ShapeDtypeStruct((2 * SLOT, width), BF16),
            jax.ShapeDtypeStruct((width // 2, 4 * width), BF16),
            jax.ShapeDtypeStruct((width // 2, 4 * width), BF16),
        ),
        in_specs=[SMEM] + [VMEM] * 7,
        out_specs=(VMEM,) * 5,
        scratch_shapes=[
            pltpu.VMEM((width, TOK), BF16),
            pltpu.VMEM((width, TOK), BF16),
            pltpu.VMEM((TOK, 3 * width), BF16),
        ],
        compiler_params=pltpu.CompilerParams(vmem_limit_bytes=56 * 1024 * 1024),
        name="window_attention",
    )(core, stay, lon, lat, gain, w, m, bias)


def finish_kernel(
    place_ref,
    x_ref,
    u_ref,
    stay_ref,
    lat_ref,
    lon_ref,
    gain_ref,
    merge_gain_ref,
    own_weight_ref,
    other_weight_ref,
    grad_ref,
    merged_ref,
):
    width = x_ref.shape[-1]
    x = x_ref[...].astype(F32)
    row = lax.broadcasted_iota(jnp.int32, (TOK, 4 * SLOT), 0)
    column = lax.broadcasted_iota(jnp.int32, (TOK, 4 * SLOT), 1)
    gather = one_hot(row_of_place(cell_of_slot(column, True)), row)
    stay, lon, lat = (r[...].astype(F32) for r in (stay_ref, lon_ref, lat_ref))
    arrays = []
    for array in range(2):
        at = slice(SLOT * array, SLOT * array + SLOT)
        later = slice(SLOT * array + 2 * SLOT, SLOT * array + 3 * SLOT)
        arrays.append(nn(gather, stacked([lat[later], lat[at], lon[at], stay[at]])))
    normalized, inverse = layer_norm(x)
    scaled = arrays[1] * gain_ref[...]
    first = jnp.mean(scaled, axis=-1, keepdims=True)
    second = jnp.mean(scaled * normalized, axis=-1, keepdims=True)
    back = inverse * (scaled - first - normalized * second)
    block = (x + arrays[0]).astype(BF16)
    grad_ref[...] = (u_ref[...].astype(F32) + back).astype(BF16)
    new = lax.broadcasted_iota(jnp.int32, (width, width), 1)
    old = lax.broadcasted_iota(jnp.int32, (width, width), 0)
    half = width // 2
    odd = (new >= half).astype(jnp.int32)
    local = new & (half - 1)
    block = nn(block, one_hot(((local >> 6) << 7) + (odd << 6) + (local & 63), old)).astype(BF16)
    row = lax.broadcasted_iota(jnp.int32, (4 * SLOT, TOK), 0)
    column = lax.broadcasted_iota(jnp.int32, (4 * SLOT, TOK), 1)
    corner, cell = row // SLOT, row % SLOT
    pair, level = cell // 2, cell % 2
    lat_at, lon_at = 2 * (pair // 6) + corner % 2, 2 * (pair % 6) + corner // 2
    place = (lat_at * WIN_LON + lon_at) * 2 + level
    corners = quarters_of(nn(one_hot(jnp.where(cell < PART, place, -1), column), block))
    joined = jnp.concatenate([c[:, :half] for c in corners] + [c[:, half:] for c in corners], axis=-1)
    features, _ = layer_norm(joined)
    features = features * merge_gain_ref[...]
    even, odds = features[:, : 2 * width], features[:, 2 * width :]
    moved = jnp.concatenate([even[:, 64:], even[:, :64]], axis=-1)

    def blocks(start):
        return jnp.where(start == 0, even, jnp.where(start == 1, odds, moved)).astype(BF16)

    core, high = place_ref[0], place_ref[1]
    merged = nn(blocks(high + core), own_weight_ref[...])
    merged = merged + nn(blocks(high + 1 - core), other_weight_ref[...])
    merged_ref[...] = merged[:PART].astype(BF16)


def finish(place, x, u, stay, lat, lon, gain, merge_gain, own_weight, other_weight):
    width = x.shape[1]
    merge_gain = merge_gain.reshape(4, width // 128, 2, 64).transpose(2, 0, 1, 3).reshape(1, -1)
    return pl.pallas_call(
        finish_kernel,
        out_shape=(
            jax.ShapeDtypeStruct(x.shape, BF16),
            jax.ShapeDtypeStruct((PART, own_weight.shape[1]), BF16),
        ),
        in_specs=[SMEM] + [VMEM] * 9,
        out_specs=(VMEM,) * 2,
        compiler_params=pltpu.CompilerParams(vmem_limit_bytes=16 * 1024 * 1024),
        name="finish",
    )(place, x, u, stay, lat, lon, gain, merge_gain, own_weight, other_weight)


def shifted(array, axis, by):
    size = lax.axis_size(axis)
    return lax.ppermute(array, axis, [(i, (i + by) % size) for i in range(size)])


def exchanged(array, axes, groups):
    return lax.all_to_all(array, axes, 0, 0, axis_index_groups=groups, tiled=True)


def plane_groups(lon_size):
    return [[4 * j + r for j in range(lon_size // 4)] for r in range(4)]


def reduce_over_planes(paired):
    lon_size = lax.axis_size("lon")
    terms = exchanged(paired, "lon", plane_groups(lon_size))
    return terms.reshape(lon_size // 4, 2, -1, paired.shape[1])


def reduce_along_z(terms):
    lon_size, lat_size = lax.axis_size("lon"), lax.axis_size("lat")
    _, _, rows, columns = terms.shape
    planes = jnp.sum(terms.astype(F32), axis=0).astype(BF16)
    planes = planes.reshape(2, rows, lat_size, columns // lat_size).transpose(0, 2, 1, 3)
    planes = planes.reshape(2 * lat_size, rows, columns // lat_size)
    groups = [
        [level * lon_size + o + 2 * high for high in range(2) for level in range(lat_size)]
        for o in range(lon_size)
        if not o & 2
    ]
    terms = exchanged(planes, ("lat", "lon"), groups)
    return jnp.sum(terms.astype(F32), axis=0).astype(BF16)


def spread_over_lat(part):
    lat_size, rows = lax.axis_size("lat"), part.shape[0]
    parts = exchanged(jnp.broadcast_to(part[None], (lat_size,) + part.shape), "lat", None)
    return parts.transpose(1, 0, 2).reshape(rows, -1)


def on_device(
    latent,
    upstream,
    norm_gain,
    heads_weight,
    mixing_weight,
    bias_table,
    bias_index,
    regions,
    merge_gain,
    merge_weight,
):
    level_count, lat_count, lon_count, width = latent.shape
    lat_total = lat_count * lax.axis_size("lat")
    token_total = level_count * lat_total * lon_count * lax.axis_size("lon")
    factor = float(token_total) ** (-0.5)
    lon_size = lax.axis_size("lon")
    lon_at = lax.axis_index("lon")
    core = (lon_at % 2).astype(jnp.int32)
    high = (lon_at // 2 % 2).astype(jnp.int32)
    first_core = core == 0
    between_cores = [(i, i ^ 1) for i in range(lon_size)]
    to_chip = [(i, (i - 1) % lon_size) for i in range(0, lon_size, 2)]
    to_core = [(i, i - 1) for i in range(1, lon_size, 2)]
    x = latent.transpose(1, 2, 0, 3).reshape(TOK, width)
    u = upstream.transpose(1, 2, 0, 3).reshape(TOK, width)
    lon_half, lat_half, stay = prepare(x, u)
    lat_global = lax.axis_index("lat") * lat_count + lax.broadcasted_iota(
        jnp.int32, regions.shape, 1
    )
    level_local = lax.broadcasted_iota(jnp.int32, regions.shape, 0)
    groups = (
        regions
        + 3 * (lat_global >= lat_total - WIN_LAT // 2).astype(jnp.int32)
        + 6 * (level_local >= LEVELS - 1).astype(jnp.int32)
    )
    operands = bias_operands(bias_table, bias_index, groups)
    with jax.named_scope("weight_core"):
        other = lax.ppermute(merge_weight, "lon", between_cores)
    pair = jnp.concatenate(
        [jnp.where(first_core, merge_weight, other), jnp.where(first_core, other, merge_weight)]
    )
    with jax.named_scope("lon_core"):
        from_core = lax.ppermute(lon_half, "lon", to_core)
    with jax.named_scope("lon_cross"):
        from_chip = lax.ppermute(jnp.concatenate([lon_half, pair]), "lon", to_chip)
    bias = gather_bias(operands)
    half_rows = lon_half.shape[0]
    lon_half = jnp.where(first_core, from_core, from_chip[:half_rows])
    pair = jnp.where(first_core, pair, from_chip[half_rows:])
    lat_half = jnp.concatenate([lat_half, lon_half[: 2 * SLOT]])
    lat_half, pair, bias = lax.optimization_barrier((lat_half, pair, bias))
    with jax.named_scope("lat_roll"):
        lat_half = shifted(lat_half, "lat", -1)
    pair = jnp.broadcast_to(pair[None], (lon_size // 4,) + pair.shape).reshape(-1, width)
    with jax.named_scope("weight_plane"):
        own_weight = exchanged(pair, "lon", plane_groups(lon_size))
    gain = norm_gain[None]
    lat_back, lon_back, stay_back, keep, send = attention(
        core.reshape(1), stay, lon_half, lat_half, gain, heads_weight, mixing_weight, bias
    )
    send, own_weight = lax.optimization_barrier((send, own_weight))
    with jax.named_scope("term_core"):
        arrived = lax.ppermute(send, "lon", between_cores)
    with jax.named_scope("weight_other"):
        other_weight = lax.ppermute(own_weight, "lon", between_cores)
    paired = (keep.astype(F32) + arrived.astype(F32)).astype(BF16)
    with jax.named_scope("term_plane"):
        terms = reduce_over_planes(paired)
    with jax.named_scope("lon_back"):
        lon_back = shifted(lon_back, "lon", 1)
    with jax.named_scope("lat_back"):
        lat_back = shifted(jnp.concatenate([lat_back, lon_back[2 * SLOT :]]), "lat", 1)
    latent_grad, merged = finish(
        jnp.stack([core, high]),
        x,
        u,
        stay_back,
        lat_back,
        lon_back[: 2 * SLOT],
        gain,
        merge_gain,
        own_weight,
        other_weight,
    )
    with jax.named_scope("term_z"):
        part = reduce_along_z(terms)
    with jax.named_scope("term_lat"):
        rows = spread_over_lat(part).astype(F32) * factor
    merged = merged.reshape(lat_count // 2, lon_count // 2, level_count, -1).transpose(2, 0, 1, 3)
    latent_grad = latent_grad.reshape(lat_count, lon_count, level_count, width)
    latent_grad = latent_grad.transpose(2, 0, 1, 3)
    return merged, latent_grad, rows[:, : 3 * width], rows[:, 3 * width :]


def solution(mesh):
    placed = (
        P(None, "lat", "lon", None),
        P(None, "lat", "lon", None),
        P(),
        P(),
        P(),
        P(),
        P(None, "lat", None, None),
        P(None, "lat", "lon"),
        P(),
        P("lon", None),
    )
    return jax.shard_map(
        on_device,
        mesh=mesh,
        in_specs=placed,
        out_specs=(
            P(None, "lat", "lon", None),
            P(None, "lat", "lon", None),
            P("lon", None),
            P("lon", None),
        ),
        check_vma=False,
    )
```

```python
import functools

import jax
import jax.numpy as jnp
from jax import lax
from jax.experimental import pallas as pl
from jax.experimental.pallas import tpu as pltpu
from jax.sharding import PartitionSpec as P

HEADS = 16
HEAD_DIM = 32
LEVELS = 2
WIN_LAT = 6
WIN_LON = 12
TOK = 144
HALF_LAT = 3
HALF_LON = 6
PART = 36
SLOT = 40
EPSILON = 1e-05
MASKED = -1e30
F32, BF16 = jnp.float32, jnp.bfloat16
VMEM = pl.BlockSpec(memory_space=pltpu.VMEM)
SMEM = pl.BlockSpec(memory_space=pltpu.SMEM)


def nn(a, b):
    return lax.dot_general(a, b, (((1,), (0,)), ((), ())), preferred_element_type=F32)


def nt(a, b):
    return lax.dot_general(a, b, (((1,), (1,)), ((), ())), preferred_element_type=F32)


def layer_norm(values):
    average = jnp.mean(values, axis=-1, keepdims=True)
    centred = values - average
    variance = jnp.mean(centred * centred, axis=-1, keepdims=True)
    inverse = lax.rsqrt(variance + EPSILON)
    return centred * inverse, inverse


def one_hot(source, old):
    return jnp.where(source == old, 1.0, 0.0).astype(BF16)


def own_cell(row):
    cell, level = row // 2, row % 2
    return cell // WIN_LON, cell % WIN_LON, level


def window_cell(place):
    level, rest = place // (TOK // 2), place % (TOK // 2)
    lat, lon = rest // WIN_LON, rest % WIN_LON
    return lat // HALF_LAT, lon // HALF_LON, lat % HALF_LAT, lon % HALF_LON, 1 - level


def picks(size, columns, source):
    row = lax.broadcasted_iota(jnp.int32, (size, 1), 0)
    column = lax.broadcasted_iota(jnp.int32, (size, columns), 1)
    return one_hot(source(row), column)


def picked_into(size, columns, target):
    row = lax.broadcasted_iota(jnp.int32, (size, columns), 0)
    column = lax.broadcasted_iota(jnp.int32, (1, columns), 1)
    return one_hot(row, target(column))


def lookup(index, table_ref):
    high, low = index >> 7, index & 127
    found = [jnp.zeros(index.shape, F32) for _ in range(HEADS)]
    for chunk in range(table_ref.shape[1] // 128):
        here = high == chunk
        for head in range(HEADS):
            row = table_ref[head : head + 1, chunk * 128 : chunk * 128 + 128]
            row = jnp.broadcast_to(row, index.shape)
            value = jnp.take_along_axis(row, low, axis=1, mode="promise_in_bounds")
            found[head] = jnp.where(here, value, found[head])
    return found


def bias_kernel(turn_ref, index_ref, table_ref, key_group_ref, query_group_ref, *refs):
    given_ref = refs[0] if len(refs) == 3 else None
    bias_ref, tail_ref = refs[-2:]
    rest = TOK - 128
    per_row = 128 // rest

    def allowed(base, start):
        return key_group_ref[pl.ds(base, 8), :] == query_group_ref[:, start : start + 128]

    def main_rows(step, carry):
        base = pl.multiple_of(step * 8, 8)
        open_pairs = allowed(base, 0)
        for head, value in enumerate(lookup(index_ref[pl.ds(base, 8), :], table_ref)):
            bias_ref[head, pl.ds(base, 8), :128] = jnp.where(open_pairs, value, MASKED)
        return carry

    def tail_rows(step, carry):
        base = pl.multiple_of(step * 8, 8)
        for head, value in enumerate(lookup(index_ref[pl.ds(TOK + base, 8), :], table_ref)):
            tail_ref[head, pl.ds(base, 8), :] = value
        return carry

    def spread_rows(step, carry):
        base = pl.multiple_of(step * 8, 8)
        open_pairs = allowed(base, 128)
        sublane = lax.broadcasted_iota(jnp.int32, (8, 128), 0)
        lane = lax.broadcasted_iota(jnp.int32, (8, 128), 1)
        place = sublane * rest + (lane & (rest - 1))
        for head in range(HEADS):
            row = jnp.broadcast_to(tail_ref[head, pl.ds(step, 1), :], (8, 128))
            value = jnp.take_along_axis(row, place, axis=1, mode="promise_in_bounds")
            value = jnp.where(open_pairs, value, MASKED)
            bias_ref[head, pl.ds(base, 8), 128:] = value[:, :rest]
        return carry

    @pl.when(turn_ref[0] == 1)
    def _():
        lax.fori_loop(0, TOK // 8, main_rows, 0)
        lax.fori_loop(0, tail_ref.shape[1] // 8, tail_rows, 0)
        lax.fori_loop(0, TOK // per_row, spread_rows, 0)

    if given_ref is not None:

        @pl.when(turn_ref[0] != 1)
        def _():
            for head in range(HEADS):
                bias_ref[head] = given_ref[head]


def bias_operands(bias_table, bias_index, groups):
    rows = bias_table.shape[0]
    padded = -(-rows // 128) * 128
    table = jnp.pad(bias_table.T, ((0, 0), (0, padded - rows)))
    index = bias_index.reshape(TOK, TOK).T
    tail = index[:, 128:].reshape(-1, 128)
    tail = jnp.pad(tail, ((0, -tail.shape[0] % 8), (0, 0)))
    index = jnp.concatenate([index[:, :128], tail])
    flat = groups.reshape(TOK)
    key_group = jnp.broadcast_to(flat[:, None], (TOK, 128))
    query_group = jnp.pad(flat, (0, 256 - TOK))[None]
    return index, table, key_group, query_group


def gather_bias(turn, operands, *given):
    tail = operands[0].shape[0] - TOK
    return pl.pallas_call(
        bias_kernel,
        out_shape=jax.ShapeDtypeStruct((HEADS, TOK, TOK), F32),
        in_specs=[SMEM] + [VMEM] * (4 + len(given)),
        out_specs=VMEM,
        scratch_shapes=[pltpu.VMEM((HEADS, tail, 128), F32)],
        compiler_params=pltpu.CompilerParams(vmem_limit_bytes=12 * 1024 * 1024),
        name="bias_gather",
    )(turn, *operands, *given)


def attention_kernel(
    core_ref,
    x_ref,
    u_ref,
    lon_ref,
    lat_ref,
    gain_ref,
    w_ref,
    m_ref,
    bias_ref,
    lat_out_ref,
    lon_out_ref,
    stay_out_ref,
    keep_ref,
    send_ref,
    ct_ref,
    dqt_ref,
    tg_ref,
):
    width = gain_ref.shape[1]
    scale = HEAD_DIM ** (-0.5)
    core = core_ref[0]

    def from_own(place):
        south, east, lat, lon, level = window_cell(place)
        row = ((lat + HALF_LAT) * WIN_LON + lon + HALF_LON) * 2 + level
        return jnp.where(south + east == 0, row, -1)

    def from_lon(array, place):
        south, east, lat, lon, level = window_cell(place)
        row = ((lat + HALF_LAT) * HALF_LON + lon) * 2 + level + 2 * PART * array
        return jnp.where((south == 0) & (east == 1), row, -1)

    def from_lat(array, place):
        south, east, lat, lon, level = window_cell(place)
        row = (lat * HALF_LON + lon) * 2 + level + PART * array + 2 * PART * east
        return jnp.where(south == 1, row, -1)

    arrays = []
    for array, own_ref in enumerate((x_ref, u_ref)):
        values = nn(picks(TOK, TOK, from_own), own_ref[...])
        values += nn(picks(TOK, TOK, functools.partial(from_lon, array)), lon_ref[...])
        values += nn(picks(TOK, TOK, functools.partial(from_lat, array)), lat_ref[...])
        arrays.append(values.astype(BF16))
    x, u = arrays
    standard, _ = layer_norm(x.astype(F32))
    xn = (standard * gain_ref[...]).astype(BF16)
    w = w_ref[...]
    m = m_ref[...]
    q_nat = nn(xn, w[:, :width]).astype(BF16)
    k_nat = nn(xn, w[:, width : 2 * width]).astype(BF16)
    v_nat = nn(xn, w[:, 2 * width :]).astype(BF16)
    row = lax.broadcasted_iota(jnp.int32, (width, width), 0)
    column = lax.broadcasted_iota(jnp.int32, (width, width), 1)
    wide_eye = one_hot(row, column)
    qt, kt, vt = (block.astype(F32).T.astype(BF16) for block in (q_nat, k_nat, v_nat))
    cg_nat = nt(u, m).astype(BF16)
    cgt = nt(m, u).astype(BF16)
    lane = lax.broadcasted_iota(jnp.int32, (TOK, 128), 1)
    for group in range(HEADS // 4):
        cut = slice(128 * group, 128 * group + 128)
        kg, vg, qg, cgg = k_nat[:, cut], v_nat[:, cut], q_nat[:, cut], cg_nat[:, cut]
        qtg, cgtg = qt[cut], cgt[cut]
        masks = [(lane >= HEAD_DIM * p) & (lane < HEAD_DIM * (p + 1)) for p in range(4)]

        def spread_heads(block):
            block = block.astype(F32)
            return jnp.concatenate([jnp.where(m_, block, 0.0) for m_ in masks]).astype(BF16)

        group_logits = nn(spread_heads(kg), qtg)
        group_grads = nn(spread_heads(vg), cgtg)
        dk = jnp.zeros((TOK, 128), F32)
        dv = jnp.zeros((TOK, 128), F32)
        for part in range(4):
            head = 4 * group + part
            own = (lane >= HEAD_DIM * part) & (lane < HEAD_DIM * (part + 1))

            def only(block):
                return jnp.where(own, block.astype(F32), 0.0).astype(BF16)

            at = slice(HEAD_DIM * head, HEAD_DIM * head + HEAD_DIM)
            logits = group_logits[TOK * part : TOK * part + TOK] * scale + bias_ref[head]
            top = jnp.max(logits, axis=0, keepdims=True)
            raised = jnp.exp(logits - top)
            shares = raised * (1.0 / jnp.sum(raised, axis=0, keepdims=True))
            shares_low = shares.astype(BF16)
            ct_ref[at, :] = nn(vt[at], shares_low).astype(BF16)
            share_grad = group_grads[TOK * part : TOK * part + TOK]
            product = shares * share_grad
            total = jnp.sum(product, axis=0, keepdims=True)
            logit_grad = (shares * (share_grad - total)).astype(BF16)
            dqt_ref[at, :] = (nn(kt[at], logit_grad) * scale).astype(BF16)
            dv = dv + nn(shares_low, only(cgg))
            dk = dk + nn(logit_grad, only(qg))
        tg_ref[:, width + 128 * group : width + 128 * group + 128] = (dk * scale).astype(BF16)
        tg_ref[:, 2 * width + 128 * group : 2 * width + 128 * group + 128] = dv.astype(BF16)
    row = lax.broadcasted_iota(jnp.int32, (TOK, TOK), 0)
    column = lax.broadcasted_iota(jnp.int32, (TOK, TOK), 1)
    eye = one_hot(row, column)
    tg_ref[:, :width] = dqt_ref[...].astype(F32).T.astype(BF16)
    ct = ct_ref[...]
    context = ct.astype(F32).T.astype(BF16)
    tg = tg_ref[...]

    def to_stay(array, place):
        south, east, lat, lon, level = window_cell(place)
        row = (lat * HALF_LON + lon) * 2 + level + PART * array
        return jnp.where(south + east == 0, row, -1)

    def to_lon(array, place):
        south, east, lat, lon, level = window_cell(place)
        row = ((lat + HALF_LAT * south) * HALF_LON + lon) * 2 + level + 2 * PART * array
        return jnp.where(east == 1, row, -1)

    def to_lat(array, place):
        south, east, lat, lon, level = window_cell(place)
        row = (lat * HALF_LON + lon) * 2 + level + PART * array
        return jnp.where((south == 1) & (east == 0), row, -1)

    results = [values.astype(BF16) for values in (nn(context, m), nt(tg, w))]
    for target, place in ((stay_out_ref, to_stay), (lon_out_ref, to_lon), (lat_out_ref, to_lat)):
        rows = target.shape[0]
        values = nn(picked_into(rows, TOK, functools.partial(place, 0)), results[0])
        values += nn(picked_into(rows, TOK, functools.partial(place, 1)), results[1])
        target[...] = values.astype(BF16)
    half = width // 2
    new = lax.broadcasted_iota(jnp.int32, (width, 1), 0)
    old = lax.broadcasted_iota(jnp.int32, (width, width), 1)
    local = new & (half - 1)
    parity = jnp.where(new >= half, 1 - core, core)
    order = one_hot(((local >> 3) << 4) + (parity << 3) + (local & 7), old)
    xnt = nt(order, xn).astype(BF16)
    cto = nn(order, ct).astype(BF16)
    for rows, target in ((slice(0, half), keep_ref), (slice(half, width), send_ref)):
        target[:, : 3 * width] = nn(xnt[rows], tg).astype(BF16)
        target[:, 3 * width :] = nn(cto[rows], u).astype(BF16)


def attention(core, x, u, lon, lat, gain, w, m, bias):
    width = gain.shape[1]
    return pl.pallas_call(
        attention_kernel,
        out_shape=(
            jax.ShapeDtypeStruct((2 * PART, width), BF16),
            jax.ShapeDtypeStruct((4 * PART, width), BF16),
            jax.ShapeDtypeStruct((2 * PART, width), BF16),
            jax.ShapeDtypeStruct((width // 2, 4 * width), BF16),
            jax.ShapeDtypeStruct((width // 2, 4 * width), BF16),
        ),
        in_specs=[SMEM] + [VMEM] * 8,
        out_specs=(VMEM,) * 5,
        scratch_shapes=[
            pltpu.VMEM((width, TOK), BF16),
            pltpu.VMEM((width, TOK), BF16),
            pltpu.VMEM((TOK, 3 * width), BF16),
        ],
        compiler_params=pltpu.CompilerParams(vmem_limit_bytes=56 * 1024 * 1024),
        name="window_attention",
    )(core, x, u, lon, lat, gain, w, m, bias)


def finish_kernel(
    place_ref,
    x_ref,
    u_ref,
    stay_ref,
    lat_ref,
    lon_ref,
    gain_ref,
    merge_gain_ref,
    own_weight_ref,
    other_weight_ref,
    grad_ref,
    merged_ref,
):
    width = x_ref.shape[-1]
    x = x_ref[...].astype(F32)

    def from_stay(array, row):
        lat, lon, level = own_cell(row)
        source = ((lat - HALF_LAT) * HALF_LON + lon - HALF_LON) * 2 + level + PART * array
        return jnp.where((lat >= HALF_LAT) & (lon >= HALF_LON), source, -1)

    def from_lon(array, row):
        lat, lon, level = own_cell(row)
        source = ((lat - HALF_LAT) * HALF_LON + lon) * 2 + level + 2 * PART * array
        return jnp.where((lat >= HALF_LAT) & (lon < HALF_LON), source, -1)

    def from_lat(array, row):
        lat, lon, level = own_cell(row)
        west = (lon < HALF_LON).astype(jnp.int32)
        place = lon - HALF_LON * (1 - west)
        source = (lat * HALF_LON + place) * 2 + level + PART * array + 2 * PART * west
        return jnp.where(lat < HALF_LAT, source, -1)

    arrays = []
    for array in range(2):
        values = 0.0
        for ref, source in ((stay_ref, from_stay), (lon_ref, from_lon), (lat_ref, from_lat)):
            taken = picks(TOK, ref.shape[0], functools.partial(source, array))
            values = values + nn(taken, ref[...])
        arrays.append(values)
    normalized, inverse = layer_norm(x)
    scaled = arrays[1] * gain_ref[...]
    first = jnp.mean(scaled, axis=-1, keepdims=True)
    second = jnp.mean(scaled * normalized, axis=-1, keepdims=True)
    back = inverse * (scaled - first - normalized * second)
    block = (x + arrays[0]).astype(BF16)
    grad_ref[...] = (u_ref[...].astype(F32) + back).astype(BF16)
    new = lax.broadcasted_iota(jnp.int32, (1, width), 1)
    old = lax.broadcasted_iota(jnp.int32, (width, width), 0)
    half = width // 2
    odd = (new >= half).astype(jnp.int32)
    local = new & (half - 1)
    block = nn(block, one_hot(((local >> 6) << 7) + (odd << 6) + (local & 63), old)).astype(BF16)
    row = lax.broadcasted_iota(jnp.int32, (4 * SLOT, 1), 0)
    column = lax.broadcasted_iota(jnp.int32, (4 * SLOT, TOK), 1)
    corner, cell = row // SLOT, row % SLOT
    pair, level = cell // 2, cell % 2
    lat_at, lon_at = 2 * (pair // 6) + corner % 2, 2 * (pair % 6) + corner // 2
    place = (lat_at * WIN_LON + lon_at) * 2 + level
    corners = nn(one_hot(jnp.where(cell < PART, place, -1), column), block)
    corners = [corners[SLOT * c : SLOT * c + SLOT] for c in range(4)]
    joined = jnp.concatenate([c[:, :half] for c in corners] + [c[:, half:] for c in corners], axis=-1)
    features, _ = layer_norm(joined)
    features = features * merge_gain_ref[...]
    even, odds = features[:, : 2 * width], features[:, 2 * width :]
    moved = jnp.concatenate([even[:, 64:], even[:, :64]], axis=-1)

    def blocks(start):
        return jnp.where(start == 0, even, jnp.where(start == 1, odds, moved)).astype(BF16)

    core, high = place_ref[0], place_ref[1]
    merged = nn(blocks(high + core), own_weight_ref[...])
    merged = merged + nn(blocks(high + 1 - core), other_weight_ref[...])
    merged_ref[...] = merged[:PART].astype(BF16)


def finish(place, x, u, stay, lat, lon, gain, merge_gain, own_weight, other_weight):
    width = x.shape[1]
    merge_gain = merge_gain.reshape(4, width // 128, 2, 64).transpose(2, 0, 1, 3).reshape(1, -1)
    return pl.pallas_call(
        finish_kernel,
        out_shape=(
            jax.ShapeDtypeStruct(x.shape, BF16),
            jax.ShapeDtypeStruct((PART, own_weight.shape[1]), BF16),
        ),
        in_specs=[SMEM] + [VMEM] * 9,
        out_specs=(VMEM,) * 2,
        compiler_params=pltpu.CompilerParams(vmem_limit_bytes=16 * 1024 * 1024),
        name="finish",
    )(place, x, u, stay, lat, lon, gain, merge_gain, own_weight, other_weight)


def shifted(array, axis, by):
    size = lax.axis_size(axis)
    return lax.ppermute(array, axis, [(i, (i + by) % size) for i in range(size)])


def exchanged(array, axes, groups):
    return lax.all_to_all(array, axes, 0, 0, axis_index_groups=groups, tiled=True)


def plane_groups(lon_size):
    return [[4 * j + r for j in range(lon_size // 4)] for r in range(4)]


def reduce_over_planes(paired):
    lon_size = lax.axis_size("lon")
    terms = exchanged(paired, "lon", plane_groups(lon_size))
    return terms.reshape(lon_size // 4, 2, -1, paired.shape[1])


def reduce_along_z(terms):
    lon_size, lat_size = lax.axis_size("lon"), lax.axis_size("lat")
    _, _, rows, columns = terms.shape
    planes = jnp.sum(terms.astype(F32), axis=0).astype(BF16)
    planes = planes.reshape(2, rows, lat_size, columns // lat_size).transpose(0, 2, 1, 3)
    planes = planes.reshape(2 * lat_size, rows, columns // lat_size)
    groups = [
        [level * lon_size + o + 2 * high for high in range(2) for level in range(lat_size)]
        for o in range(lon_size)
        if not o & 2
    ]
    terms = exchanged(planes, ("lat", "lon"), groups)
    return jnp.sum(terms.astype(F32), axis=0).astype(BF16)


def spread_over_lat(part):
    lat_size, rows = lax.axis_size("lat"), part.shape[0]
    parts = exchanged(jnp.broadcast_to(part[None], (lat_size,) + part.shape), "lat", None)
    return parts.transpose(1, 0, 2).reshape(rows, -1)


def on_device(
    latent,
    upstream,
    norm_gain,
    heads_weight,
    mixing_weight,
    bias_table,
    bias_index,
    regions,
    merge_gain,
    merge_weight,
):
    level_count, lat_count, lon_count, width = latent.shape
    lat_total = lat_count * lax.axis_size("lat")
    token_total = level_count * lat_total * lon_count * lax.axis_size("lon")
    factor = float(token_total) ** (-0.5)
    lon_size = lax.axis_size("lon")
    lon_at = lax.axis_index("lon")
    core = (lon_at % 2).astype(jnp.int32)
    high = (lon_at // 2 % 2).astype(jnp.int32)
    first_core = core == 0
    between_cores = [(i, i ^ 1) for i in range(lon_size)]
    to_chip = [(i, (i - 1) % lon_size) for i in range(0, lon_size, 2)]
    to_core = [(i, i - 1) for i in range(1, lon_size, 2)]

    def rows_of(block):
        return block.transpose(1, 2, 0, 3).reshape(-1, width)

    x, u = rows_of(latent), rows_of(upstream)
    lon_half = [rows_of(array[:, :, :HALF_LON]) for array in (latent, upstream)]
    lat_half = [rows_of(array[:, :HALF_LAT, HALF_LON:]) for array in (latent, upstream)]
    lon_half = jnp.concatenate(lon_half)
    lat_global = lax.axis_index("lat") * lat_count + lax.broadcasted_iota(
        jnp.int32, regions.shape, 1
    )
    level_local = lax.broadcasted_iota(jnp.int32, regions.shape, 0)
    groups = (
        regions
        + 3 * (lat_global >= lat_total - WIN_LAT // 2).astype(jnp.int32)
        + 6 * (level_local >= LEVELS - 1).astype(jnp.int32)
    )
    operands = bias_operands(bias_table, bias_index, groups)
    early = ((core == 0) & (high == 0)).astype(jnp.int32).reshape(1)
    with jax.named_scope("lon_core"):
        from_core = lax.ppermute(lon_half, "lon", to_core)
    with jax.named_scope("weight_core"):
        other = lax.ppermute(merge_weight, "lon", between_cores)
    pair = [jnp.where(first_core, merge_weight, other), jnp.where(first_core, other, merge_weight)]
    leaving = jnp.concatenate([lon_half] + pair)
    early, from_core, leaving = lax.optimization_barrier((early, from_core, leaving))
    bias = gather_bias(early, operands)
    leaving, bias = lax.optimization_barrier((leaving, bias))
    with jax.named_scope("lon_cross"):
        from_chip = lax.ppermute(leaving, "lon", to_chip)
    bias = gather_bias(1 - early, operands, bias)
    half_rows = lon_half.shape[0]
    lon_half = jnp.where(first_core, from_core, from_chip[:half_rows])
    pair = jnp.where(first_core, leaving[half_rows:], from_chip[half_rows:])
    lat_half += [lon_half[:PART], lon_half[2 * PART : 3 * PART]]
    lat_half = jnp.concatenate(lat_half)
    lat_half, pair, bias = lax.optimization_barrier((lat_half, pair, bias))
    with jax.named_scope("lat_roll"):
        lat_half = shifted(lat_half, "lat", -1)
    pair = jnp.broadcast_to(pair[None], (lon_size // 4,) + pair.shape).reshape(-1, width)
    with jax.named_scope("weight_plane"):
        own_weight = exchanged(pair, "lon", plane_groups(lon_size))
    gain = norm_gain[None]
    lat_back, lon_back, stay_back, keep, send = attention(
        core.reshape(1), x, u, lon_half, lat_half, gain, heads_weight, mixing_weight, bias
    )
    send, own_weight = lax.optimization_barrier((send, own_weight))
    with jax.named_scope("term_core"):
        arrived = lax.ppermute(send, "lon", between_cores)
    paired = (keep.astype(F32) + arrived.astype(F32)).astype(BF16)
    with jax.named_scope("term_plane"):
        terms = reduce_over_planes(paired)
    with jax.named_scope("lon_back"):
        lon_back = shifted(lon_back, "lon", 1)
    with jax.named_scope("lat_back"):
        lat_back = shifted(jnp.concatenate([lat_back, lon_back[PART : 2 * PART], lon_back[3 * PART :]]), "lat", 1)
    with jax.named_scope("term_z"):
        part = reduce_along_z(terms)
    with jax.named_scope("weight_other"):
        other_weight = lax.ppermute(own_weight, "lon", between_cores)
    latent_grad, merged = finish(
        jnp.stack([core, high]),
        x,
        u,
        stay_back,
        lat_back,
        lon_back,
        gain,
        merge_gain,
        own_weight,
        other_weight,
    )
    with jax.named_scope("term_lat"):
        rows = spread_over_lat(part).astype(F32) * factor
    merged = merged.reshape(lat_count // 2, lon_count // 2, level_count, -1).transpose(2, 0, 1, 3)
    latent_grad = latent_grad.reshape(lat_count, lon_count, level_count, width)
    latent_grad = latent_grad.transpose(2, 0, 1, 3)
    return merged, latent_grad, rows[:, : 3 * width], rows[:, 3 * width :]


def solution(mesh):
    placed = (
        P(None, "lat", "lon", None),
        P(None, "lat", "lon", None),
        P(),
        P(),
        P(),
        P(),
        P(None, "lat", None, None),
        P(None, "lat", "lon"),
        P(),
        P("lon", None),
    )
    return jax.shard_map(
        on_device,
        mesh=mesh,
        in_specs=placed,
        out_specs=(
            P(None, "lat", "lon", None),
            P(None, "lat", "lon", None),
            P("lon", None),
            P("lon", None),
        ),
        check_vma=False,
    )
```

```python
import functools

import jax
import jax.numpy as jnp
from jax import lax
from jax.experimental import pallas as pl
from jax.experimental.pallas import tpu as pltpu
from jax.sharding import PartitionSpec as P

HEADS = 16
HEAD_DIM = 32
LEVELS = 2
WIN_LAT = 6
WIN_LON = 12
TOK = 144
HALF_LAT = 3
HALF_LON = 6
PART = 36
SLOT = 40
EPSILON = 1e-05
MASKED = -1e30
F32, BF16 = jnp.float32, jnp.bfloat16
VMEM = pl.BlockSpec(memory_space=pltpu.VMEM)
SMEM = pl.BlockSpec(memory_space=pltpu.SMEM)


def nn(a, b):
    return lax.dot_general(a, b, (((1,), (0,)), ((), ())), preferred_element_type=F32)


def nt(a, b):
    return lax.dot_general(a, b, (((1,), (1,)), ((), ())), preferred_element_type=F32)


def layer_norm(values):
    average = jnp.mean(values, axis=-1, keepdims=True)
    centred = values - average
    variance = jnp.mean(centred * centred, axis=-1, keepdims=True)
    inverse = lax.rsqrt(variance + EPSILON)
    return centred * inverse, inverse


def one_hot(source, old):
    return jnp.where(source == old, 1.0, 0.0).astype(BF16)


def own_cell(row):
    cell, level = row // 2, row % 2
    return cell // WIN_LON, cell % WIN_LON, level


def window_cell(place):
    level, rest = place // (TOK // 2), place % (TOK // 2)
    lat, lon = rest // WIN_LON, rest % WIN_LON
    return lat // HALF_LAT, lon // HALF_LON, lat % HALF_LAT, lon % HALF_LON, 1 - level


def picks(size, columns, source):
    row = lax.broadcasted_iota(jnp.int32, (size, 1), 0)
    column = lax.broadcasted_iota(jnp.int32, (size, columns), 1)
    return one_hot(source(row), column)


def picked_into(size, columns, target):
    row = lax.broadcasted_iota(jnp.int32, (size, columns), 0)
    column = lax.broadcasted_iota(jnp.int32, (1, columns), 1)
    return one_hot(row, target(column))


def lookup(index, table_ref):
    high, low = index >> 7, index & 127
    found = [jnp.zeros(index.shape, F32) for _ in range(HEADS)]
    for chunk in range(table_ref.shape[1] // 128):
        here = high == chunk
        for head in range(HEADS):
            row = table_ref[head : head + 1, chunk * 128 : chunk * 128 + 128]
            row = jnp.broadcast_to(row, index.shape)
            value = jnp.take_along_axis(row, low, axis=1, mode="promise_in_bounds")
            found[head] = jnp.where(here, value, found[head])
    return found


def bias_kernel(turn_ref, index_ref, table_in_ref, key_group_ref, query_group_ref, *refs):
    given_ref = refs[0] if len(refs) == 4 else None
    bias_ref, tail_ref, table_ref = refs[-3:]
    rest = TOK - 128
    per_row = 128 // rest

    def allowed(base, start):
        return key_group_ref[pl.ds(base, 8), :] == query_group_ref[:, start : start + 128]

    def main_rows(step, carry):
        base = pl.multiple_of(step * 8, 8)
        open_pairs = allowed(base, 0)
        for head, value in enumerate(lookup(index_ref[pl.ds(base, 8), :], table_ref)):
            bias_ref[head, pl.ds(base, 8), :128] = jnp.where(open_pairs, value, MASKED)
        return carry

    def tail_rows(step, carry):
        base = pl.multiple_of(step * 8, 8)
        for head, value in enumerate(lookup(index_ref[pl.ds(TOK + base, 8), :], table_ref)):
            tail_ref[head, pl.ds(base, 8), :] = value
        return carry

    def spread_rows(step, carry):
        base = pl.multiple_of(step * 8, 8)
        open_pairs = allowed(base, 128)
        sublane = lax.broadcasted_iota(jnp.int32, (8, 128), 0)
        lane = lax.broadcasted_iota(jnp.int32, (8, 128), 1)
        place = sublane * rest + (lane & (rest - 1))
        for head in range(HEADS):
            row = jnp.broadcast_to(tail_ref[head, pl.ds(step, 1), :], (8, 128))
            value = jnp.take_along_axis(row, place, axis=1, mode="promise_in_bounds")
            value = jnp.where(open_pairs, value, MASKED)
            bias_ref[head, pl.ds(base, 8), 128:] = value[:, :rest]
        return carry

    @pl.when(turn_ref[0] == 1)
    def _():
        table_ref[:, : table_in_ref.shape[1]] = table_in_ref[...]
        lax.fori_loop(0, TOK // 8, main_rows, 0)
        lax.fori_loop(0, tail_ref.shape[1] // 8, tail_rows, 0)
        lax.fori_loop(0, TOK // per_row, spread_rows, 0)

    if given_ref is not None:

        @pl.when(turn_ref[0] != 1)
        def _():
            for head in range(HEADS):
                bias_ref[head] = given_ref[head]


def bias_operands(bias_table, bias_index, groups):
    table = bias_table.T
    index = bias_index.reshape(TOK, TOK).T
    tail = index[:, 128:].reshape(-1, 128)
    tail = jnp.pad(tail, ((0, -tail.shape[0] % 8), (0, 0)))
    index = jnp.concatenate([index[:, :128], tail])
    flat = groups.reshape(TOK)
    key_group = jnp.broadcast_to(flat[:, None], (TOK, 128))
    query_group = jnp.pad(flat, (0, 256 - TOK))[None]
    return index, table, key_group, query_group


def gather_bias(turn, operands, *given):
    tail = operands[0].shape[0] - TOK
    table_width = -(-operands[1].shape[1] // 128) * 128
    return pl.pallas_call(
        bias_kernel,
        out_shape=jax.ShapeDtypeStruct((HEADS, TOK, TOK), F32),
        in_specs=[SMEM] + [VMEM] * (4 + len(given)),
        out_specs=VMEM,
        scratch_shapes=[
            pltpu.VMEM((HEADS, tail, 128), F32),
            pltpu.VMEM((HEADS, table_width), F32),
        ],
        compiler_params=pltpu.CompilerParams(vmem_limit_bytes=12 * 1024 * 1024),
        name="bias_gather",
    )(turn, *operands, *given)


def attention_kernel(
    core_ref,
    x_ref,
    u_ref,
    lon_ref,
    lat_ref,
    gain_ref,
    w_ref,
    m_ref,
    bias_ref,
    lat_out_ref,
    lon_out_ref,
    stay_out_ref,
    keep_ref,
    send_ref,
    ct_ref,
    dqt_ref,
    tg_ref,
):
    width = gain_ref.shape[1]
    scale = HEAD_DIM ** (-0.5)
    core = core_ref[0]

    def from_own(place):
        south, east, lat, lon, level = window_cell(place)
        row = ((lat + HALF_LAT) * WIN_LON + lon + HALF_LON) * 2 + level
        return jnp.where(south + east == 0, row, -1)

    def from_lon(array, place):
        south, east, lat, lon, level = window_cell(place)
        row = ((lat + HALF_LAT) * HALF_LON + lon) * 2 + level + 2 * PART * array
        return jnp.where((south == 0) & (east == 1), row, -1)

    def from_lat(array, place):
        south, east, lat, lon, level = window_cell(place)
        row = (lat * HALF_LON + lon) * 2 + level + PART * array + 2 * PART * east
        return jnp.where(south == 1, row, -1)

    arrays = []
    for array, own_ref in enumerate((x_ref, u_ref)):
        values = nn(picks(TOK, TOK, from_own), own_ref[...])
        values += nn(picks(TOK, TOK, functools.partial(from_lon, array)), lon_ref[...])
        values += nn(picks(TOK, TOK, functools.partial(from_lat, array)), lat_ref[...])
        arrays.append(values.astype(BF16))
    x, u = arrays
    standard, _ = layer_norm(x.astype(F32))
    xn = (standard * gain_ref[...]).astype(BF16)
    w = w_ref[...]
    m = m_ref[...]
    q_nat = nn(xn, w[:, :width]).astype(BF16)
    k_nat = nn(xn, w[:, width : 2 * width]).astype(BF16)
    v_nat = nn(xn, w[:, 2 * width :]).astype(BF16)
    row = lax.broadcasted_iota(jnp.int32, (width, width), 0)
    column = lax.broadcasted_iota(jnp.int32, (width, width), 1)
    wide_eye = one_hot(row, column)
    qt, kt, vt = (block.astype(F32).T.astype(BF16) for block in (q_nat, k_nat, v_nat))
    cg_nat = nt(u, m).astype(BF16)
    cgt = nt(m, u).astype(BF16)
    lane = lax.broadcasted_iota(jnp.int32, (TOK, 128), 1)
    for group in range(HEADS // 4):
        cut = slice(128 * group, 128 * group + 128)
        kg, vg, qg, cgg = k_nat[:, cut], v_nat[:, cut], q_nat[:, cut], cg_nat[:, cut]
        qtg, cgtg = qt[cut], cgt[cut]
        masks = [(lane >= HEAD_DIM * p) & (lane < HEAD_DIM * (p + 1)) for p in range(4)]

        def spread_heads(block):
            block = block.astype(F32)
            return jnp.concatenate([jnp.where(m_, block, 0.0) for m_ in masks]).astype(BF16)

        group_logits = nn(spread_heads(kg), qtg)
        group_grads = nn(spread_heads(vg), cgtg)
        dk = jnp.zeros((TOK, 128), F32)
        dv = jnp.zeros((TOK, 128), F32)
        for part in range(4):
            head = 4 * group + part
            own = (lane >= HEAD_DIM * part) & (lane < HEAD_DIM * (part + 1))

            def only(block):
                return jnp.where(own, block.astype(F32), 0.0).astype(BF16)

            at = slice(HEAD_DIM * head, HEAD_DIM * head + HEAD_DIM)
            logits = group_logits[TOK * part : TOK * part + TOK] * scale + bias_ref[head]
            top = jnp.max(logits, axis=0, keepdims=True)
            raised = jnp.exp(logits - top)
            shares = raised * (1.0 / jnp.sum(raised, axis=0, keepdims=True))
            shares_low = shares.astype(BF16)
            ct_ref[at, :] = nn(vt[at], shares_low).astype(BF16)
            share_grad = group_grads[TOK * part : TOK * part + TOK]
            product = shares * share_grad
            total = jnp.sum(product, axis=0, keepdims=True)
            logit_grad = (shares * (share_grad - total)).astype(BF16)
            dqt_ref[at, :] = (nn(kt[at], logit_grad) * scale).astype(BF16)
            dv = dv + nn(shares_low, only(cgg))
            dk = dk + nn(logit_grad, only(qg))
        tg_ref[:, width + 128 * group : width + 128 * group + 128] = (dk * scale).astype(BF16)
        tg_ref[:, 2 * width + 128 * group : 2 * width + 128 * group + 128] = dv.astype(BF16)
    row = lax.broadcasted_iota(jnp.int32, (TOK, TOK), 0)
    column = lax.broadcasted_iota(jnp.int32, (TOK, TOK), 1)
    eye = one_hot(row, column)
    tg_ref[:, :width] = dqt_ref[...].astype(F32).T.astype(BF16)
    ct = ct_ref[...]
    context = ct.astype(F32).T.astype(BF16)
    tg = tg_ref[...]

    def to_stay(array, place):
        south, east, lat, lon, level = window_cell(place)
        row = (lat * HALF_LON + lon) * 2 + level + PART * array
        return jnp.where(south + east == 0, row, -1)

    def to_lon(array, place):
        south, east, lat, lon, level = window_cell(place)
        row = ((lat + HALF_LAT * south) * HALF_LON + lon) * 2 + level + 2 * PART * array
        return jnp.where(east == 1, row, -1)

    def to_lat(array, place):
        south, east, lat, lon, level = window_cell(place)
        row = (lat * HALF_LON + lon) * 2 + level + PART * array
        return jnp.where((south == 1) & (east == 0), row, -1)

    results = [values.astype(BF16) for values in (nn(context, m), nt(tg, w))]
    for target, place in ((stay_out_ref, to_stay), (lon_out_ref, to_lon), (lat_out_ref, to_lat)):
        rows = target.shape[0]
        values = nn(picked_into(rows, TOK, functools.partial(place, 0)), results[0])
        values += nn(picked_into(rows, TOK, functools.partial(place, 1)), results[1])
        target[...] = values.astype(BF16)
    half = width // 2
    new = lax.broadcasted_iota(jnp.int32, (width, 1), 0)
    old = lax.broadcasted_iota(jnp.int32, (width, width), 1)
    local = new & (half - 1)
    parity = jnp.where(new >= half, 1 - core, core)
    order = one_hot(((local >> 3) << 4) + (parity << 3) + (local & 7), old)
    xnt = nt(order, xn).astype(BF16)
    cto = nn(order, ct).astype(BF16)
    for rows, target in ((slice(0, half), keep_ref), (slice(half, width), send_ref)):
        target[:, : 3 * width] = nn(xnt[rows], tg).astype(BF16)
        target[:, 3 * width :] = nn(cto[rows], u).astype(BF16)


def attention(core, x, u, lon, lat, gain, w, m, bias):
    width = gain.shape[1]
    return pl.pallas_call(
        attention_kernel,
        out_shape=(
            jax.ShapeDtypeStruct((2 * PART, width), BF16),
            jax.ShapeDtypeStruct((4 * PART, width), BF16),
            jax.ShapeDtypeStruct((2 * PART, width), BF16),
            jax.ShapeDtypeStruct((width // 2, 4 * width), BF16),
            jax.ShapeDtypeStruct((width // 2, 4 * width), BF16),
        ),
        in_specs=[SMEM] + [VMEM] * 8,
        out_specs=(VMEM,) * 5,
        scratch_shapes=[
            pltpu.VMEM((width, TOK), BF16),
            pltpu.VMEM((width, TOK), BF16),
            pltpu.VMEM((TOK, 3 * width), BF16),
        ],
        compiler_params=pltpu.CompilerParams(vmem_limit_bytes=56 * 1024 * 1024),
        name="window_attention",
    )(core, x, u, lon, lat, gain, w, m, bias)


def finish_kernel(
    place_ref,
    x_ref,
    u_ref,
    stay_ref,
    lat_ref,
    lon_ref,
    gain_ref,
    merge_gain_ref,
    own_weight_ref,
    other_weight_ref,
    grad_ref,
    merged_ref,
):
    width = x_ref.shape[-1]
    x = x_ref[...].astype(F32)

    def from_stay(array, row):
        lat, lon, level = own_cell(row)
        source = ((lat - HALF_LAT) * HALF_LON + lon - HALF_LON) * 2 + level + PART * array
        return jnp.where((lat >= HALF_LAT) & (lon >= HALF_LON), source, -1)

    def from_lon(array, row):
        lat, lon, level = own_cell(row)
        source = ((lat - HALF_LAT) * HALF_LON + lon) * 2 + level + 2 * PART * array
        return jnp.where((lat >= HALF_LAT) & (lon < HALF_LON), source, -1)

    def from_lat(array, row):
        lat, lon, level = own_cell(row)
        west = (lon < HALF_LON).astype(jnp.int32)
        place = lon - HALF_LON * (1 - west)
        source = (lat * HALF_LON + place) * 2 + level + PART * array + 2 * PART * west
        return jnp.where(lat < HALF_LAT, source, -1)

    arrays = []
    for array in range(2):
        values = 0.0
        for ref, source in ((stay_ref, from_stay), (lon_ref, from_lon), (lat_ref, from_lat)):
            taken = picks(TOK, ref.shape[0], functools.partial(source, array))
            values = values + nn(taken, ref[...])
        arrays.append(values)
    normalized, inverse = layer_norm(x)
    scaled = arrays[1] * gain_ref[...]
    first = jnp.mean(scaled, axis=-1, keepdims=True)
    second = jnp.mean(scaled * normalized, axis=-1, keepdims=True)
    back = inverse * (scaled - first - normalized * second)
    block = (x + arrays[0]).astype(BF16)
    grad_ref[...] = (u_ref[...].astype(F32) + back).astype(BF16)
    new = lax.broadcasted_iota(jnp.int32, (1, width), 1)
    old = lax.broadcasted_iota(jnp.int32, (width, width), 0)
    half = width // 2
    odd = (new >= half).astype(jnp.int32)
    local = new & (half - 1)
    block = nn(block, one_hot(((local >> 6) << 7) + (odd << 6) + (local & 63), old)).astype(BF16)
    row = lax.broadcasted_iota(jnp.int32, (4 * SLOT, 1), 0)
    column = lax.broadcasted_iota(jnp.int32, (4 * SLOT, TOK), 1)
    corner, cell = row // SLOT, row % SLOT
    pair, level = cell // 2, cell % 2
    lat_at, lon_at = 2 * (pair // 6) + corner % 2, 2 * (pair % 6) + corner // 2
    place = (lat_at * WIN_LON + lon_at) * 2 + level
    corners = nn(one_hot(jnp.where(cell < PART, place, -1), column), block)
    corners = [corners[SLOT * c : SLOT * c + SLOT] for c in range(4)]
    joined = jnp.concatenate([c[:, :half] for c in corners] + [c[:, half:] for c in corners], axis=-1)
    features, _ = layer_norm(joined)
    features = features * merge_gain_ref[...]
    even, odds = features[:, : 2 * width], features[:, 2 * width :]
    moved = jnp.concatenate([even[:, 64:], even[:, :64]], axis=-1)

    def blocks(start):
        return jnp.where(start == 0, even, jnp.where(start == 1, odds, moved)).astype(BF16)

    core, high = place_ref[0], place_ref[1]
    merged = nn(blocks(high + core), own_weight_ref[...])
    merged = merged + nn(blocks(high + 1 - core), other_weight_ref[...])
    merged_ref[...] = merged[:PART].astype(BF16)


def finish(place, x, u, stay, lat, lon, gain, merge_gain, own_weight, other_weight):
    width = x.shape[1]
    merge_gain = merge_gain.reshape(4, width // 128, 2, 64).transpose(2, 0, 1, 3).reshape(1, -1)
    return pl.pallas_call(
        finish_kernel,
        out_shape=(
            jax.ShapeDtypeStruct(x.shape, BF16),
            jax.ShapeDtypeStruct((PART, own_weight.shape[1]), BF16),
        ),
        in_specs=[SMEM] + [VMEM] * 9,
        out_specs=(VMEM,) * 2,
        compiler_params=pltpu.CompilerParams(vmem_limit_bytes=16 * 1024 * 1024),
        name="finish",
    )(place, x, u, stay, lat, lon, gain, merge_gain, own_weight, other_weight)


def shifted(array, axis, by):
    size = lax.axis_size(axis)
    return lax.ppermute(array, axis, [(i, (i + by) % size) for i in range(size)])


def exchanged(array, axes, groups):
    return lax.all_to_all(array, axes, 0, 0, axis_index_groups=groups, tiled=True)


def plane_groups(lon_size):
    return [[4 * j + r for j in range(lon_size // 4)] for r in range(4)]


def reduce_over_planes(paired):
    lon_size = lax.axis_size("lon")
    terms = exchanged(paired, "lon", plane_groups(lon_size))
    return terms.reshape(lon_size // 4, 2, -1, paired.shape[1])


def reduce_along_z(terms):
    lon_size, lat_size = lax.axis_size("lon"), lax.axis_size("lat")
    _, _, rows, columns = terms.shape
    planes = jnp.sum(terms.astype(F32), axis=0).astype(BF16)
    planes = planes.reshape(2, rows, lat_size, columns // lat_size).transpose(0, 2, 1, 3)
    planes = planes.reshape(2 * lat_size, rows, columns // lat_size)
    groups = [
        [level * lon_size + o + 2 * high for high in range(2) for level in range(lat_size)]
        for o in range(lon_size)
        if not o & 2
    ]
    terms = exchanged(planes, ("lat", "lon"), groups)
    return jnp.sum(terms.astype(F32), axis=0).astype(BF16)


def spread_over_lat(part):
    lat_size, rows = lax.axis_size("lat"), part.shape[0]
    parts = exchanged(jnp.broadcast_to(part[None], (lat_size,) + part.shape), "lat", None)
    return parts.transpose(1, 0, 2).reshape(rows, -1)


def on_device(
    latent,
    upstream,
    norm_gain,
    heads_weight,
    mixing_weight,
    bias_table,
    bias_index,
    regions,
    merge_gain,
    merge_weight,
):
    level_count, lat_count, lon_count, width = latent.shape
    lat_total = lat_count * lax.axis_size("lat")
    token_total = level_count * lat_total * lon_count * lax.axis_size("lon")
    factor = float(token_total) ** (-0.5)
    lon_size = lax.axis_size("lon")
    lon_at = lax.axis_index("lon")
    core = (lon_at % 2).astype(jnp.int32)
    high = (lon_at // 2 % 2).astype(jnp.int32)
    first_core = core == 0
    between_cores = [(i, i ^ 1) for i in range(lon_size)]
    to_chip = [(i, (i - 1) % lon_size) for i in range(0, lon_size, 2)]
    to_core = [(i, i - 1) for i in range(1, lon_size, 2)]

    def rows_of(block):
        return block.transpose(1, 2, 0, 3).reshape(-1, width)

    lon_half = jnp.concatenate([rows_of(array[:, :, :HALF_LON]) for array in (latent, upstream)])
    lat_global = lax.axis_index("lat") * lat_count + lax.broadcasted_iota(
        jnp.int32, regions.shape, 1
    )
    level_local = lax.broadcasted_iota(jnp.int32, regions.shape, 0)
    groups = (
        regions
        + 3 * (lat_global >= lat_total - WIN_LAT // 2).astype(jnp.int32)
        + 6 * (level_local >= LEVELS - 1).astype(jnp.int32)
    )
    operands = bias_operands(bias_table, bias_index, groups)
    early = ((core == 0) & (high == 0)).astype(jnp.int32).reshape(1)
    with jax.named_scope("lon_core"):
        from_core = lax.ppermute(lon_half, "lon", to_core)
    with jax.named_scope("weight_core"):
        other = lax.ppermute(merge_weight, "lon", between_cores)
    pair = [jnp.where(first_core, merge_weight, other), jnp.where(first_core, other, merge_weight)]
    leaving = jnp.concatenate([lon_half] + pair)
    early, from_core, leaving = lax.optimization_barrier((early, from_core, leaving))
    bias = gather_bias(early, operands)
    leaving, bias, latent, upstream = lax.optimization_barrier((leaving, bias, latent, upstream))
    x, u = rows_of(latent), rows_of(upstream)
    lat_half = [rows_of(array[:, :HALF_LAT, HALF_LON:]) for array in (latent, upstream)]
    with jax.named_scope("lon_cross"):
        from_chip = lax.ppermute(leaving, "lon", to_chip)
    bias = gather_bias(1 - early, operands, bias)
    half_rows = lon_half.shape[0]
    lon_half = jnp.where(first_core, from_core, from_chip[:half_rows])
    pair = jnp.where(first_core, leaving[half_rows:], from_chip[half_rows:])
    lat_half += [lon_half[:PART], lon_half[2 * PART : 3 * PART]]
    lat_half = jnp.concatenate(lat_half)
    lat_half, pair, bias = lax.optimization_barrier((lat_half, pair, bias))
    with jax.named_scope("lat_roll"):
        lat_half = shifted(lat_half, "lat", -1)
    pair = jnp.broadcast_to(pair[None], (lon_size // 4,) + pair.shape).reshape(-1, width)
    with jax.named_scope("weight_plane"):
        own_weight = exchanged(pair, "lon", plane_groups(lon_size))
    gain = norm_gain[None]
    lat_back, lon_back, stay_back, keep, send = attention(
        core.reshape(1), x, u, lon_half, lat_half, gain, heads_weight, mixing_weight, bias
    )
    send, own_weight = lax.optimization_barrier((send, own_weight))
    with jax.named_scope("term_core"):
        arrived = lax.ppermute(send, "lon", between_cores)
    paired = (keep.astype(F32) + arrived.astype(F32)).astype(BF16)
    with jax.named_scope("term_plane"):
        terms = reduce_over_planes(paired)
    with jax.named_scope("lon_back"):
        lon_back = shifted(lon_back, "lon", 1)
    with jax.named_scope("lat_back"):
        lat_back = shifted(jnp.concatenate([lat_back, lon_back[PART : 2 * PART], lon_back[3 * PART :]]), "lat", 1)
    with jax.named_scope("term_z"):
        part = reduce_along_z(terms)
    with jax.named_scope("weight_other"):
        other_weight = lax.ppermute(own_weight, "lon", between_cores)
    latent_grad, merged = finish(
        jnp.stack([core, high]),
        x,
        u,
        stay_back,
        lat_back,
        lon_back,
        gain,
        merge_gain,
        own_weight,
        other_weight,
    )
    with jax.named_scope("term_lat"):
        rows = spread_over_lat(part).astype(F32) * factor
    merged = merged.reshape(lat_count // 2, lon_count // 2, level_count, -1).transpose(2, 0, 1, 3)
    latent_grad = latent_grad.reshape(lat_count, lon_count, level_count, width)
    latent_grad = latent_grad.transpose(2, 0, 1, 3)
    return merged, latent_grad, rows[:, : 3 * width], rows[:, 3 * width :]


def solution(mesh):
    placed = (
        P(None, "lat", "lon", None),
        P(None, "lat", "lon", None),
        P(),
        P(),
        P(),
        P(),
        P(None, "lat", None, None),
        P(None, "lat", "lon"),
        P(),
        P("lon", None),
    )
    return jax.shard_map(
        on_device,
        mesh=mesh,
        in_specs=placed,
        out_specs=(
            P(None, "lat", "lon", None),
            P(None, "lat", "lon", None),
            P("lon", None),
            P("lon", None),
        ),
        check_vma=False,
    )
```

```python
import functools

import jax
import jax.numpy as jnp
from jax import lax
from jax.experimental import pallas as pl
from jax.experimental.pallas import tpu as pltpu
from jax.sharding import PartitionSpec as P

HEADS = 16
HEAD_DIM = 32
LEVELS = 2
WIN_LAT = 6
WIN_LON = 12
TOK = 144
HALF_LAT = 3
HALF_LON = 6
PART = 36
SLOT = 40
EPSILON = 1e-05
MASKED = -1e30
F32, BF16 = jnp.float32, jnp.bfloat16
VMEM = pl.BlockSpec(memory_space=pltpu.VMEM)
SMEM = pl.BlockSpec(memory_space=pltpu.SMEM)


def nn(a, b):
    return lax.dot_general(a, b, (((1,), (0,)), ((), ())), preferred_element_type=F32)


def nt(a, b):
    return lax.dot_general(a, b, (((1,), (1,)), ((), ())), preferred_element_type=F32)


def layer_norm(values):
    average = jnp.mean(values, axis=-1, keepdims=True)
    centred = values - average
    variance = jnp.mean(centred * centred, axis=-1, keepdims=True)
    inverse = lax.rsqrt(variance + EPSILON)
    return centred * inverse, inverse


def one_hot(source, old):
    return jnp.where(source == old, 1.0, 0.0).astype(BF16)


def own_cell(row):
    cell, level = row // 2, row % 2
    return cell // WIN_LON, cell % WIN_LON, level


def window_cell(place):
    level, rest = place // (TOK // 2), place % (TOK // 2)
    lat, lon = rest // WIN_LON, rest % WIN_LON
    return lat // HALF_LAT, lon // HALF_LON, lat % HALF_LAT, lon % HALF_LON, 1 - level


def picks(size, columns, source):
    row = lax.broadcasted_iota(jnp.int32, (size, 1), 0)
    column = lax.broadcasted_iota(jnp.int32, (size, columns), 1)
    return one_hot(source(row), column)


def picked_into(size, columns, target):
    row = lax.broadcasted_iota(jnp.int32, (size, columns), 0)
    column = lax.broadcasted_iota(jnp.int32, (1, columns), 1)
    return one_hot(row, target(column))


def lookup(index, table_ref):
    high, low = index >> 7, index & 127
    found = [jnp.zeros(index.shape, F32) for _ in range(HEADS)]
    for chunk in range(table_ref.shape[1] // 128):
        here = high == chunk
        for head in range(HEADS):
            row = table_ref[head : head + 1, chunk * 128 : chunk * 128 + 128]
            row = jnp.broadcast_to(row, index.shape)
            value = jnp.take_along_axis(row, low, axis=1, mode="promise_in_bounds")
            found[head] = jnp.where(here, value, found[head])
    return found


def bias_kernel(turn_ref, index_ref, table_in_ref, key_group_ref, query_group_ref, *refs):
    given_ref = refs[0] if len(refs) == 4 else None
    bias_ref, tail_ref, table_ref = refs[-3:]
    rest = TOK - 128
    per_row = 128 // rest

    def allowed(base, start):
        return key_group_ref[pl.ds(base, 8), :] == query_group_ref[:, start : start + 128]

    def main_rows(step, carry):
        base = pl.multiple_of(step * 8, 8)
        open_pairs = allowed(base, 0)
        for head, value in enumerate(lookup(index_ref[pl.ds(base, 8), :], table_ref)):
            bias_ref[head, pl.ds(base, 8), :128] = jnp.where(open_pairs, value, MASKED)
        return carry

    def tail_rows(step, carry):
        base = pl.multiple_of(step * 8, 8)
        for head, value in enumerate(lookup(index_ref[pl.ds(TOK + base, 8), :], table_ref)):
            tail_ref[head, pl.ds(base, 8), :] = value
        return carry

    def spread_rows(step, carry):
        base = pl.multiple_of(step * 8, 8)
        open_pairs = allowed(base, 128)
        sublane = lax.broadcasted_iota(jnp.int32, (8, 128), 0)
        lane = lax.broadcasted_iota(jnp.int32, (8, 128), 1)
        place = sublane * rest + (lane & (rest - 1))
        for head in range(HEADS):
            row = jnp.broadcast_to(tail_ref[head, pl.ds(step, 1), :], (8, 128))
            value = jnp.take_along_axis(row, place, axis=1, mode="promise_in_bounds")
            value = jnp.where(open_pairs, value, MASKED)
            bias_ref[head, pl.ds(base, 8), 128:] = value[:, :rest]
        return carry

    @pl.when(turn_ref[0] == 1)
    def _():
        table_ref[:, : table_in_ref.shape[1]] = table_in_ref[...]
        lax.fori_loop(0, TOK // 8, main_rows, 0)
        lax.fori_loop(0, tail_ref.shape[1] // 8, tail_rows, 0)
        lax.fori_loop(0, TOK // per_row, spread_rows, 0)

    if given_ref is not None:

        @pl.when(turn_ref[0] != 1)
        def _():
            for head in range(HEADS):
                bias_ref[head] = given_ref[head]


def bias_operands(bias_table, bias_index, groups):
    table = bias_table.T
    index = bias_index.reshape(TOK, TOK).T
    tail = index[:, 128:].reshape(-1, 128)
    tail = jnp.pad(tail, ((0, -tail.shape[0] % 8), (0, 0)))
    index = jnp.concatenate([index[:, :128], tail])
    flat = groups.reshape(TOK)
    key_group = jnp.broadcast_to(flat[:, None], (TOK, 128))
    query_group = jnp.pad(flat, (0, 256 - TOK))[None]
    return index, table, key_group, query_group


def gather_bias(turn, operands, *given):
    tail = operands[0].shape[0] - TOK
    table_width = -(-operands[1].shape[1] // 128) * 128
    return pl.pallas_call(
        bias_kernel,
        out_shape=jax.ShapeDtypeStruct((HEADS, TOK, TOK), F32),
        in_specs=[SMEM] + [VMEM] * (4 + len(given)),
        out_specs=VMEM,
        scratch_shapes=[
            pltpu.VMEM((HEADS, tail, 128), F32),
            pltpu.VMEM((HEADS, table_width), F32),
        ],
        compiler_params=pltpu.CompilerParams(vmem_limit_bytes=12 * 1024 * 1024),
        name="bias_gather",
    )(turn, *operands, *given)


def attention_kernel(
    core_ref,
    x_ref,
    u_ref,
    lon_ref,
    lat_ref,
    gain_ref,
    w_ref,
    m_ref,
    bias_ref,
    lat_out_ref,
    lon_out_ref,
    stay_out_ref,
    keep_ref,
    send_ref,
    ct_ref,
    dqt_ref,
    tg_ref,
):
    width = gain_ref.shape[1]
    scale = HEAD_DIM ** (-0.5)
    core = core_ref[0]

    def from_own(place):
        south, east, lat, lon, level = window_cell(place)
        row = ((lat + HALF_LAT) * WIN_LON + lon + HALF_LON) * 2 + level
        return jnp.where(south + east == 0, row, -1)

    def from_lon(array, place):
        south, east, lat, lon, level = window_cell(place)
        row = ((lat + HALF_LAT) * HALF_LON + lon) * 2 + level + 2 * PART * array
        return jnp.where((south == 0) & (east == 1), row, -1)

    def from_lat(array, place):
        south, east, lat, lon, level = window_cell(place)
        row = (lat * HALF_LON + lon) * 2 + level + PART * array + 2 * PART * east
        return jnp.where(south == 1, row, -1)

    arrays = []
    for array, own_ref in enumerate((x_ref, u_ref)):
        values = nn(picks(TOK, TOK, from_own), own_ref[...])
        values += nn(picks(TOK, TOK, functools.partial(from_lon, array)), lon_ref[...])
        values += nn(picks(TOK, TOK, functools.partial(from_lat, array)), lat_ref[...])
        arrays.append(values.astype(BF16))
    x, u = arrays
    standard, _ = layer_norm(x.astype(F32))
    xn = (standard * gain_ref[...]).astype(BF16)
    w = w_ref[...]
    m = m_ref[...]
    q_nat = nn(xn, w[:, :width]).astype(BF16)
    k_nat = nn(xn, w[:, width : 2 * width]).astype(BF16)
    v_nat = nn(xn, w[:, 2 * width :]).astype(BF16)
    row = lax.broadcasted_iota(jnp.int32, (width, width), 0)
    column = lax.broadcasted_iota(jnp.int32, (width, width), 1)
    wide_eye = one_hot(row, column)
    qt, kt, vt = (block.astype(F32).T.astype(BF16) for block in (q_nat, k_nat, v_nat))
    cg_nat = nt(u, m).astype(BF16)
    cgt = nt(m, u).astype(BF16)
    lane = lax.broadcasted_iota(jnp.int32, (TOK, 128), 1)
    for group in range(HEADS // 4):
        cut = slice(128 * group, 128 * group + 128)
        kg, vg, qg, cgg = k_nat[:, cut], v_nat[:, cut], q_nat[:, cut], cg_nat[:, cut]
        qtg, cgtg = qt[cut], cgt[cut]
        masks = [(lane >= HEAD_DIM * p) & (lane < HEAD_DIM * (p + 1)) for p in range(4)]

        def spread_heads(block):
            block = block.astype(F32)
            return jnp.concatenate([jnp.where(m_, block, 0.0) for m_ in masks]).astype(BF16)

        group_logits = nn(spread_heads(kg), qtg)
        group_grads = nn(spread_heads(vg), cgtg)
        dk = jnp.zeros((TOK, 128), F32)
        dv = jnp.zeros((TOK, 128), F32)
        for part in range(4):
            head = 4 * group + part
            own = (lane >= HEAD_DIM * part) & (lane < HEAD_DIM * (part + 1))

            def only(block):
                return jnp.where(own, block.astype(F32), 0.0).astype(BF16)

            at = slice(HEAD_DIM * head, HEAD_DIM * head + HEAD_DIM)
            logits = group_logits[TOK * part : TOK * part + TOK] * scale + bias_ref[head]
            top = jnp.max(logits, axis=0, keepdims=True)
            raised = jnp.exp(logits - top)
            shares = raised * (1.0 / jnp.sum(raised, axis=0, keepdims=True))
            shares_low = shares.astype(BF16)
            ct_ref[at, :] = nn(vt[at], shares_low).astype(BF16)
            share_grad = group_grads[TOK * part : TOK * part + TOK]
            product = shares * share_grad
            total = jnp.sum(product, axis=0, keepdims=True)
            logit_grad = (shares * (share_grad - total)).astype(BF16)
            dqt_ref[at, :] = (nn(kt[at], logit_grad) * scale).astype(BF16)
            dv = dv + nn(shares_low, only(cgg))
            dk = dk + nn(logit_grad, only(qg))
        tg_ref[:, width + 128 * group : width + 128 * group + 128] = (dk * scale).astype(BF16)
        tg_ref[:, 2 * width + 128 * group : 2 * width + 128 * group + 128] = dv.astype(BF16)
    row = lax.broadcasted_iota(jnp.int32, (TOK, TOK), 0)
    column = lax.broadcasted_iota(jnp.int32, (TOK, TOK), 1)
    eye = one_hot(row, column)
    tg_ref[:, :width] = dqt_ref[...].astype(F32).T.astype(BF16)
    ct = ct_ref[...]
    context = ct.astype(F32).T.astype(BF16)
    tg = tg_ref[...]

    def to_stay(array, place):
        south, east, lat, lon, level = window_cell(place)
        row = (lat * HALF_LON + lon) * 2 + level + PART * array
        return jnp.where(south + east == 0, row, -1)

    def to_lon(array, place):
        south, east, lat, lon, level = window_cell(place)
        row = ((lat + HALF_LAT * south) * HALF_LON + lon) * 2 + level + 2 * PART * array
        return jnp.where(east == 1, row, -1)

    def to_lat(array, place):
        south, east, lat, lon, level = window_cell(place)
        row = (lat * HALF_LON + lon) * 2 + level + PART * array
        return jnp.where((south == 1) & (east == 0), row, -1)

    results = [values.astype(BF16) for values in (nn(context, m), nt(tg, w))]
    for target, place in ((stay_out_ref, to_stay), (lon_out_ref, to_lon), (lat_out_ref, to_lat)):
        rows = target.shape[0]
        values = nn(picked_into(rows, TOK, functools.partial(place, 0)), results[0])
        values += nn(picked_into(rows, TOK, functools.partial(place, 1)), results[1])
        target[...] = values.astype(BF16)
    half = width // 2
    new = lax.broadcasted_iota(jnp.int32, (width, 1), 0)
    old = lax.broadcasted_iota(jnp.int32, (width, width), 1)
    local = new & (half - 1)
    parity = jnp.where(new >= half, 1 - core, core)
    order = one_hot(((local >> 3) << 4) + (parity << 3) + (local & 7), old)
    xnt = nt(order, xn).astype(BF16)
    cto = nn(order, ct).astype(BF16)
    for rows, target in ((slice(0, half), keep_ref), (slice(half, width), send_ref)):
        target[:, : 3 * width] = nn(xnt[rows], tg).astype(BF16)
        target[:, 3 * width :] = nn(cto[rows], u).astype(BF16)


def attention(core, x, u, lon, lat, gain, w, m, bias):
    width = gain.shape[1]
    return pl.pallas_call(
        attention_kernel,
        out_shape=(
            jax.ShapeDtypeStruct((2 * PART, width), BF16),
            jax.ShapeDtypeStruct((4 * PART, width), BF16),
            jax.ShapeDtypeStruct((2 * PART, width), BF16),
            jax.ShapeDtypeStruct((width // 2, 4 * width), BF16),
            jax.ShapeDtypeStruct((width // 2, 4 * width), BF16),
        ),
        in_specs=[SMEM] + [VMEM] * 8,
        out_specs=(VMEM,) * 5,
        scratch_shapes=[
            pltpu.VMEM((width, TOK), BF16),
            pltpu.VMEM((width, TOK), BF16),
            pltpu.VMEM((TOK, 3 * width), BF16),
        ],
        compiler_params=pltpu.CompilerParams(vmem_limit_bytes=56 * 1024 * 1024),
        name="window_attention",
    )(core, x, u, lon, lat, gain, w, m, bias)


def finish_kernel(
    place_ref,
    x_ref,
    u_ref,
    stay_ref,
    lat_ref,
    lon_ref,
    gain_ref,
    merge_gain_ref,
    own_weight_ref,
    other_weight_ref,
    grad_ref,
    merged_ref,
):
    width = x_ref.shape[-1]
    x = x_ref[...].astype(F32)

    def from_stay(array, row):
        lat, lon, level = own_cell(row)
        source = ((lat - HALF_LAT) * HALF_LON + lon - HALF_LON) * 2 + level + PART * array
        return jnp.where((lat >= HALF_LAT) & (lon >= HALF_LON), source, -1)

    def from_lon(array, row):
        lat, lon, level = own_cell(row)
        source = ((lat - HALF_LAT) * HALF_LON + lon) * 2 + level + 2 * PART * array
        return jnp.where((lat >= HALF_LAT) & (lon < HALF_LON), source, -1)

    def from_lat(array, row):
        lat, lon, level = own_cell(row)
        west = (lon < HALF_LON).astype(jnp.int32)
        place = lon - HALF_LON * (1 - west)
        source = (lat * HALF_LON + place) * 2 + level + PART * array + 2 * PART * west
        return jnp.where(lat < HALF_LAT, source, -1)

    arrays = []
    for array in range(2):
        values = 0.0
        for ref, source in ((stay_ref, from_stay), (lon_ref, from_lon), (lat_ref, from_lat)):
            taken = picks(TOK, ref.shape[0], functools.partial(source, array))
            values = values + nn(taken, ref[...])
        arrays.append(values)
    normalized, inverse = layer_norm(x)
    scaled = arrays[1] * gain_ref[...]
    first = jnp.mean(scaled, axis=-1, keepdims=True)
    second = jnp.mean(scaled * normalized, axis=-1, keepdims=True)
    back = inverse * (scaled - first - normalized * second)
    block = (x + arrays[0]).astype(BF16)
    grad_ref[...] = (u_ref[...].astype(F32) + back).astype(BF16)
    new = lax.broadcasted_iota(jnp.int32, (1, width), 1)
    old = lax.broadcasted_iota(jnp.int32, (width, width), 0)
    half = width // 2
    odd = (new >= half).astype(jnp.int32)
    local = new & (half - 1)
    block = nn(block, one_hot(((local >> 6) << 7) + (odd << 6) + (local & 63), old)).astype(BF16)
    row = lax.broadcasted_iota(jnp.int32, (4 * SLOT, 1), 0)
    column = lax.broadcasted_iota(jnp.int32, (4 * SLOT, TOK), 1)
    corner, cell = row // SLOT, row % SLOT
    pair, level = cell // 2, cell % 2
    lat_at, lon_at = 2 * (pair // 6) + corner % 2, 2 * (pair % 6) + corner // 2
    place = (lat_at * WIN_LON + lon_at) * 2 + level
    corners = nn(one_hot(jnp.where(cell < PART, place, -1), column), block)
    corners = [corners[SLOT * c : SLOT * c + SLOT] for c in range(4)]
    joined = jnp.concatenate([c[:, :half] for c in corners] + [c[:, half:] for c in corners], axis=-1)
    features, _ = layer_norm(joined)
    features = features * merge_gain_ref[...]
    even, odds = features[:, : 2 * width], features[:, 2 * width :]
    moved = jnp.concatenate([even[:, 64:], even[:, :64]], axis=-1)

    def blocks(start):
        return jnp.where(start == 0, even, jnp.where(start == 1, odds, moved)).astype(BF16)

    core, high = place_ref[0], place_ref[1]
    merged = nn(blocks(high + core), own_weight_ref[...])
    merged = merged + nn(blocks(high + 1 - core), other_weight_ref[...])
    merged_ref[...] = merged[:PART].astype(BF16)


def finish(place, x, u, stay, lat, lon, gain, merge_gain, own_weight, other_weight):
    width = x.shape[1]
    merge_gain = merge_gain.reshape(4, width // 128, 2, 64).transpose(2, 0, 1, 3).reshape(1, -1)
    return pl.pallas_call(
        finish_kernel,
        out_shape=(
            jax.ShapeDtypeStruct(x.shape, BF16),
            jax.ShapeDtypeStruct((PART, own_weight.shape[1]), BF16),
        ),
        in_specs=[SMEM] + [VMEM] * 9,
        out_specs=(VMEM,) * 2,
        compiler_params=pltpu.CompilerParams(vmem_limit_bytes=16 * 1024 * 1024),
        name="finish",
    )(place, x, u, stay, lat, lon, gain, merge_gain, own_weight, other_weight)


def shifted(array, axis, by):
    size = lax.axis_size(axis)
    return lax.ppermute(array, axis, [(i, (i + by) % size) for i in range(size)])


def exchanged(array, axes, groups):
    return lax.all_to_all(array, axes, 0, 0, axis_index_groups=groups, tiled=True)


def plane_groups(lon_size):
    return [[4 * j + r for j in range(lon_size // 4)] for r in range(4)]


def reduce_over_planes(paired):
    lon_size = lax.axis_size("lon")
    terms = exchanged(paired, "lon", plane_groups(lon_size))
    return terms.reshape(lon_size // 4, 2, -1, paired.shape[1])


def reduce_along_z(terms):
    lon_size, lat_size = lax.axis_size("lon"), lax.axis_size("lat")
    _, _, rows, columns = terms.shape
    planes = jnp.sum(terms.astype(F32), axis=0).astype(BF16)
    planes = planes.reshape(2, rows, lat_size, columns // lat_size).transpose(0, 2, 1, 3)
    planes = planes.reshape(2 * lat_size, rows, columns // lat_size)
    groups = [
        [level * lon_size + o + 2 * high for high in range(2) for level in range(lat_size)]
        for o in range(lon_size)
        if not o & 2
    ]
    terms = exchanged(planes, ("lat", "lon"), groups)
    return jnp.sum(terms.astype(F32), axis=0).astype(BF16)


def spread_over_lat(part):
    lat_size, rows = lax.axis_size("lat"), part.shape[0]
    parts = exchanged(jnp.broadcast_to(part[None], (lat_size,) + part.shape), "lat", None)
    return parts.transpose(1, 0, 2).reshape(rows, -1)


def on_device(
    latent,
    upstream,
    norm_gain,
    heads_weight,
    mixing_weight,
    bias_table,
    bias_index,
    regions,
    merge_gain,
    merge_weight,
):
    level_count, lat_count, lon_count, width = latent.shape
    lat_total = lat_count * lax.axis_size("lat")
    token_total = level_count * lat_total * lon_count * lax.axis_size("lon")
    factor = float(token_total) ** (-0.5)
    lon_size = lax.axis_size("lon")
    lon_at = lax.axis_index("lon")
    core = (lon_at % 2).astype(jnp.int32)
    high = (lon_at // 2 % 2).astype(jnp.int32)
    first_core = core == 0
    between_cores = [(i, i ^ 1) for i in range(lon_size)]
    to_chip = [(i, (i - 1) % lon_size) for i in range(0, lon_size, 2)]

    def rows_of(block):
        return block.transpose(1, 2, 0, 3).reshape(-1, width)

    lon_half = jnp.concatenate([rows_of(array[:, :, :HALF_LON]) for array in (latent, upstream)])
    lat_global = lax.axis_index("lat") * lat_count + lax.broadcasted_iota(
        jnp.int32, regions.shape, 1
    )
    level_local = lax.broadcasted_iota(jnp.int32, regions.shape, 0)
    groups = (
        regions
        + 3 * (lat_global >= lat_total - WIN_LAT // 2).astype(jnp.int32)
        + 6 * (level_local >= LEVELS - 1).astype(jnp.int32)
    )
    operands = bias_operands(bias_table, bias_index, groups)
    early = ((core == 0) & (high == 0)).astype(jnp.int32).reshape(1)
    half_rows = lon_half.shape[0]
    with jax.named_scope("lon_core"):
        between = lax.ppermute(jnp.concatenate([lon_half, merge_weight]), "lon", between_cores)
    from_core, other = between[:half_rows], between[half_rows:]
    pair = [jnp.where(first_core, merge_weight, other), jnp.where(first_core, other, merge_weight)]
    leaving = jnp.concatenate([lon_half] + pair)
    early, leaving = lax.optimization_barrier((early, leaving))
    bias = gather_bias(early, operands)
    leaving, bias, latent, upstream = lax.optimization_barrier((leaving, bias, latent, upstream))
    x, u = rows_of(latent), rows_of(upstream)
    lat_half = [rows_of(array[:, :HALF_LAT, HALF_LON:]) for array in (latent, upstream)]
    with jax.named_scope("lon_cross"):
        from_chip = lax.ppermute(leaving, "lon", to_chip)
    bias = gather_bias(1 - early, operands, bias)
    lon_half = jnp.where(first_core, from_core, from_chip[:half_rows])
    pair = jnp.where(first_core, leaving[half_rows:], from_chip[half_rows:])
    lat_half += [lon_half[:PART], lon_half[2 * PART : 3 * PART]]
    lat_half = jnp.concatenate(lat_half)
    lat_half, pair, bias = lax.optimization_barrier((lat_half, pair, bias))
    with jax.named_scope("lat_roll"):
        lat_half = shifted(lat_half, "lat", -1)
    pair = jnp.broadcast_to(pair[None], (lon_size // 4,) + pair.shape).reshape(-1, width)
    with jax.named_scope("weight_plane"):
        own_weight = exchanged(pair, "lon", plane_groups(lon_size))
    gain = norm_gain[None]
    lat_back, lon_back, stay_back, keep, send = attention(
        core.reshape(1), x, u, lon_half, lat_half, gain, heads_weight, mixing_weight, bias
    )
    send, own_weight = lax.optimization_barrier((send, own_weight))
    with jax.named_scope("term_core"):
        arrived = lax.ppermute(send, "lon", between_cores)
    paired = (keep.astype(F32) + arrived.astype(F32)).astype(BF16)
    with jax.named_scope("term_plane"):
        terms = reduce_over_planes(paired)
    with jax.named_scope("lon_back"):
        lon_back = shifted(lon_back, "lon", 1)
    with jax.named_scope("lat_back"):
        lat_back = shifted(jnp.concatenate([lat_back, lon_back[PART : 2 * PART], lon_back[3 * PART :]]), "lat", 1)
    with jax.named_scope("term_z"):
        part = reduce_along_z(terms)
    with jax.named_scope("weight_other"):
        other_weight = lax.ppermute(own_weight, "lon", between_cores)
    latent_grad, merged = finish(
        jnp.stack([core, high]),
        x,
        u,
        stay_back,
        lat_back,
        lon_back,
        gain,
        merge_gain,
        own_weight,
        other_weight,
    )
    with jax.named_scope("term_lat"):
        rows = spread_over_lat(part).astype(F32) * factor
    merged = merged.reshape(lat_count // 2, lon_count // 2, level_count, -1).transpose(2, 0, 1, 3)
    latent_grad = latent_grad.reshape(lat_count, lon_count, level_count, width)
    latent_grad = latent_grad.transpose(2, 0, 1, 3)
    return merged, latent_grad, rows[:, : 3 * width], rows[:, 3 * width :]


def solution(mesh):
    placed = (
        P(None, "lat", "lon", None),
        P(None, "lat", "lon", None),
        P(),
        P(),
        P(),
        P(),
        P(None, "lat", None, None),
        P(None, "lat", "lon"),
        P(),
        P("lon", None),
    )
    return jax.shard_map(
        on_device,
        mesh=mesh,
        in_specs=placed,
        out_specs=(
            P(None, "lat", "lon", None),
            P(None, "lat", "lon", None),
            P("lon", None),
            P("lon", None),
        ),
        check_vma=False,
    )
```
